128 devices in a mesh: sec: 2 (over core), dev: 64 (over x, y, z).
Axes of the slice: x: 4, y: 4, z: 4, core: 2. Of those that a mesh axis runs over, the one named last changes fastest.
Arguments:
- resid: bfloat16 [1024, 7168], P(('sec', 'dev')), may hold values from -6 to 6
- ffn_gain: float32 [7168], replicated, may hold values from 0.25 to 1.75
- expert_ids: int32 [1024, 8], P(('sec', 'dev')), may hold values from 0 to 15, all different within a row; in each aligned block of 8 rows (0 to 7, 8 to 15, ...) at most 6 rows name the same one
- gate_weights: float32 [1024, 8], P(('sec', 'dev')), may hold values from 0.1 to 0.6
- w_gate: bfloat16 [7168, 32768], P(None, ('sec', 'dev')), may hold values from -0.0625 to 0.0625
- w_up: bfloat16 [7168, 32768], P(None, ('sec', 'dev')), may hold values from -0.0625 to 0.0625
- w_down: bfloat16 [32768, 7168], P(('sec', 'dev')), may hold values from -0.125 to 0.125
- attn_gain: float32 [7168], replicated, may hold values from 0.25 to 1.75
- w_kv: bfloat16 [7168, 576], replicated, may hold values from -0.0625 to 0.0625
- kv_gain: float32 [512], replicated, may hold values from 0.25 to 1.75
- cache: bfloat16 [1024, 256, 576], P(('sec', 'dev')), may hold values from -6 to 6
- lengths: int32 [1024], P(('sec', 'dev')), may hold values from 1 to 256, as said below
- queries: bfloat16 [1024, 128, 576], P(('sec', 'dev')), may hold values from -150 to 150
Outputs:
- hidden: bfloat16 [1024, 7168], P(('sec', 'dev'))
- new_entry: bfloat16 [1024, 576], P(('sec', 'dev'))
- attn_out: bfloat16 [1024, 128, 512], P(('sec', 'dev'))
The draws below stay inside these ranges and needn't reach their ends.
Inputs may be any that keep to these rules, and one draw needn't show every extreme that they name: `expert_ids`: the 8 ids of a token differ; among the 8 tokens of one device at most 6 name the same expert, and in every draw some expert is named by exactly 6 of them. `lengths`: some request in every draw has all 256 positions cached.
All inputs are finite; a program needn't handle non-finite values.
Results may differ from the reference program's by a relative error of at most 0.011.
Values may be sent and summed in bfloat16 or wider, within the bound.
No kernel may reach another device: no remote copies, remote signals or barrier semaphores. Data moves between devices by JAX's collectives and lax.ppermute only.
A program may use at most 192 MiB of HBM per device.

```python
import math
import jax
import jax.numpy as jnp
import numpy as np
from jax import lax

D = 7168
FFW = 2048
H = 128
KVL = 512
TOP = 8
EXPERTS = 16
TOK_DEV = 8
CTX = 256
KVW = 576
CAP = 6
TOKENS = 1024
DEVICES = 128


def draw_lengths(key, part):
    key_bits = jax.random.fold_in(key, 11)
    key_vals = jax.random.fold_in(key, 12)
    key_pick = jax.random.fold_in(key, 13)
    top_bit = CTX.bit_length() - 1
    bit_count = jax.random.randint(key_bits, (TOKENS,), 0, top_bit + 1)
    upper_vals = jnp.left_shift(jnp.ones((TOKENS,), jnp.int32), bit_count.astype(jnp.int32))
    values = jax.random.randint(key_vals, (TOKENS,), 1, upper_vals + 1)
    chosen = jax.random.randint(key_pick, (), 0, TOKENS)
    values = jnp.where(jnp.arange(TOKENS) == chosen, CTX, values)
    return values.astype(jnp.int32)


def draw_queries(key, part):
    key_base = jax.random.fold_in(key, 21)
    base_vals = jax.random.normal(key_base, (TOKENS, H, KVW), jnp.float32)
    return jnp.clip(base_vals, -150.0, 150.0).astype(jnp.bfloat16)


def shard_levels(stream_key, shape, cuts, least, top_value):
    def one(axis_at, parts):
        steps = jax.random.uniform(jax.random.fold_in(jax.random.fold_in(stream_key, 6), axis_at), (parts,), jnp.float32, least / len(cuts), top_value / len(cuts))
        return jnp.repeat(jnp.exp(steps), shape[axis_at] // parts).reshape((-1,) + (1,) * (len(shape) - axis_at - 1))

    loudness = one(*cuts[0])
    for cut in cuts[1:]:
        loudness = loudness * one(*cut)
    return loudness


def routed_block(key, own, number, rows, amount, top, limit, slope):
    ranking = jax.random.permutation(key, amount)
    crowded, common = load_shares(amount, rows * top, limit, slope, True), load_shares(amount, rows * top, limit, slope, False)
    places = jnp.arange(amount)

    def named(sizes, rotation):
        used = int((sizes > 0).sum())
        fixed = max(1, used // 4)
        shifted = fixed + (places - fixed + rotation * (used - fixed)) % max(1, amount - fixed)
        return jnp.zeros((amount,), jnp.int32).at[ranking[jnp.where(places < fixed, places, shifted)]].set(jnp.asarray(sizes, jnp.int32))

    sizes = jnp.where(number % 4 == 0, named(crowded, number // 4), named(common, number - number // 4 - 1))
    mixed = jax.random.permutation(jax.random.fold_in(own, 3), amount)
    giver, sink = mixed[0:amount // 2 * 2:2], mixed[1:amount // 2 * 2:2]
    slack = jnp.minimum(sizes[giver] - 1, limit - sizes[sink]) // 2
    slack = jnp.where((giver == ranking[0]) | (sink == ranking[0]) | (sizes[sink] == 0), 0, jnp.maximum(slack, 0))
    shifted = jax.random.randint(jax.random.fold_in(own, 4), (amount // 2,), 0, 1 << 20) % (slack + 1)
    sizes = sizes.at[giver].add(-shifted).at[sink].add(shifted)
    members = jnp.searchsorted(jnp.cumsum(sizes), jnp.arange(rows * top), side="right").astype(jnp.int32)
    table = members.reshape(top, rows).T
    table = table[jax.random.permutation(jax.random.fold_in(own, 1), rows)]
    rotation = jax.random.randint(jax.random.fold_in(own, 2), (rows, 1), 0, top)
    return jnp.take_along_axis(table, (jnp.arange(top)[None, :] + rotation) % top, axis=1)


def load_shares(amount, total, reach, skew, full):
    portions = [(1 << 20) // math.isqrt(grade ** skew) + 1 for grade in range(1, amount + 1)]
    largest = reach if full else min(reach, max(-(-total // amount), total * portions[0] // sum(portions)))
    least = 1 if total - largest >= amount - 1 else 0
    holding, rest = [largest] + [least] * (amount - 1), total - largest - least * (amount - 1)
    while rest > 0:
        movable = [i for i in range(1, amount) if holding[i] < largest] or [i for i in range(1, amount) if holding[i] < reach]
        whole, remaining = sum([portions[i] for i in movable]), rest
        for i in movable:
            addition = min(reach - holding[i], max(1, remaining * portions[i] // whole), rest)
            holding[i] = holding[i] + addition
            rest = rest - addition
    return np.array(holding)


def normal_values(rng, dims, spread, reach, pieces=(), kind=jnp.bfloat16):
    result = jax.random.normal(rng, dims, jnp.float32) * spread
    if len(pieces) > 0:
        result = shard_levels(rng, dims, pieces, -0.22, 0.18) * result
    return jnp.clip(result, min=-reach, max=reach).astype(kind)


def setup_inputs(seed: int = 0) -> dict:
    arg_keys = jax.random.split(jax.random.key(seed), 14)
    resid = normal_values(arg_keys[0], (TOKENS, D), 1.0, 6.0, ((0, 128),))
    ffn_gain = jnp.clip(1.0 + 0.15 * jax.random.normal(arg_keys[1], (D,), jnp.float32), 0.25, 1.75)
    expert_ids_keys = jax.random.split(jax.random.fold_in(arg_keys[2], 1), TOKENS // TOK_DEV)
    expert_ids_turns = jax.random.permutation(jax.random.fold_in(arg_keys[2], 3), TOKENS // TOK_DEV)
    expert_ids = jax.vmap(lambda own, number: routed_block(jax.random.fold_in(arg_keys[2], 2), own, number, TOK_DEV, EXPERTS, TOP, CAP, 2))(expert_ids_keys, expert_ids_turns).reshape((TOKENS, TOP))
    gate_weights = jnp.clip(0.1 + 0.5 * jax.random.uniform(arg_keys[3], (TOKENS, TOP), jnp.float32) ** shard_levels(arg_keys[3], (TOKENS, TOP), ((0, 128),), -0.2, 0.2), 0.1, 0.6)
    w_gate = normal_values(arg_keys[4], (D, EXPERTS * FFW), D ** -0.5, 0.0625, ((1, 128),))
    w_up = normal_values(arg_keys[5], (D, EXPERTS * FFW), D ** -0.5, 0.0625, ((1, 128),))
    w_down = normal_values(arg_keys[6], (EXPERTS * FFW, D), FFW ** -0.5, 0.125, ((0, 128),))
    attn_gain = jnp.clip(1.0 + 0.15 * jax.random.normal(arg_keys[7], (D,), jnp.float32), 0.25, 1.75)
    w_kv = normal_values(arg_keys[8], (D, KVW), D ** -0.5, 0.0625)
    kv_gain = jnp.clip(1.0 + 0.15 * jax.random.normal(arg_keys[9], (KVL,), jnp.float32), 0.25, 1.75)
    cache = normal_values(arg_keys[10], (TOKENS, CTX, KVW), 1.0, 6.0, ((0, 128),))
    lengths = draw_lengths(jax.random.fold_in(arg_keys[13], 71), 0)
    queries = draw_queries(jax.random.fold_in(arg_keys[13], 71), 0)
    return {"resid": resid, "ffn_gain": ffn_gain, "expert_ids": expert_ids, "gate_weights": gate_weights, "w_gate": w_gate, "w_up": w_up, "w_down": w_down, "attn_gain": attn_gain, "w_kv": w_kv, "kv_gain": kv_gain, "cache": cache, "lengths": lengths, "queries": queries}


norm_eps = 1e-06
SCORE_SCALE = 0.0721687836

def rms_scale(values, gain_vec):
    values = values.astype(jnp.float32)
    return values * lax.rsqrt(lax.optimization_barrier(jnp.mean(values * values, axis=-1, keepdims=True)) + norm_eps) * gain_vec

def rotate_half(rotary, positions):
    half_dim = rotary.shape[-1] // 2
    inv_freq = jnp.exp(-jnp.log(10000.0) * jnp.arange(half_dim).astype(jnp.float32) * 2.0 / rotary.shape[-1])
    angles = positions.astype(jnp.float32)[:, None] * inv_freq[None, :]
    lower_half = rotary[:, :half_dim]
    upper_half = rotary[:, half_dim:]
    cosine = jnp.cos(angles)
    sine_val = jnp.sin(angles)
    return jnp.concatenate([lower_half * cosine - upper_half * sine_val, upper_half * cosine + lower_half * sine_val], axis=-1)

def reference(resid, ffn_gain, expert_ids, gate_weights, w_gate, w_up, w_down, attn_gain, w_kv, kv_gain, cache, lengths, queries):
    normed = rms_scale(resid, ffn_gain).astype(jnp.bfloat16)
    flat_ids = expert_ids.reshape(-1)
    flat_gates = gate_weights.reshape(-1)
    entry_count = flat_ids.shape[0]
    room = DEVICES * CAP

    def one_expert(total, expert):
        picked = jnp.nonzero(flat_ids == expert, size=room, fill_value=entry_count)[0]
        is_live = picked < entry_count
        safe_pick = jnp.minimum(picked, entry_count - 1)
        token_rows = (safe_pick // TOP).astype(jnp.int32)
        slot_rows = normed[token_rows]
        start = (expert * FFW).astype(jnp.int32)
        gate_cols = lax.dynamic_slice_in_dim(w_gate, start, FFW, 1)
        up_cols = lax.dynamic_slice_in_dim(w_up, start, FFW, 1)
        down_rows = lax.dynamic_slice_in_dim(w_down, start, FFW, 0)
        gate_act = jnp.dot(slot_rows, gate_cols, preferred_element_type=jnp.float32)
        up_act = jnp.dot(slot_rows, up_cols, preferred_element_type=jnp.float32)
        hidden_act = (jax.nn.silu(gate_act) * up_act).astype(jnp.bfloat16)
        produced = jnp.dot(hidden_act, down_rows, preferred_element_type=jnp.float32)
        weight = jnp.where(is_live, flat_gates[safe_pick], 0.0).astype(jnp.float32)
        return (total.at[token_rows].add(produced * weight[:, None]), None)
    moe, _ = lax.scan(one_expert, jnp.zeros((TOKENS, D), jnp.float32), jnp.arange(EXPERTS, dtype=jnp.int32))
    hidden = (resid.astype(jnp.float32) + moe).astype(jnp.bfloat16)
    attn_in = rms_scale(hidden, attn_gain).astype(jnp.bfloat16)
    kv_raw = jnp.dot(attn_in, w_kv, preferred_element_type=jnp.float32)
    latent = rms_scale(kv_raw[:, :KVL], kv_gain)
    rotated = rotate_half(kv_raw[:, KVL:], lengths)
    new_entry = jnp.concatenate([latent, rotated], axis=-1).astype(jnp.bfloat16)

    def attend(packed):
        query_row, cache_row, entry_row, length_val = packed
        query_f = query_row.astype(jnp.float32)
        cache_f = cache_row.astype(jnp.float32)
        entry_f = entry_row.astype(jnp.float32)
        scores_old = jnp.einsum('hc,pc->hp', query_f, cache_f) * SCORE_SCALE
        scores_new = jnp.einsum('hc,c->h', query_f, entry_f) * SCORE_SCALE
        live_mask = jnp.arange(CTX) < length_val
        scores_old = jnp.where(live_mask[None, :], scores_old, -jnp.inf)
        peak = jnp.maximum(lax.optimization_barrier(jnp.max(scores_old, axis=1)), scores_new)
        exp_old = jnp.exp(scores_old - peak[:, None])
        exp_new = jnp.exp(scores_new - peak)
        denom = lax.optimization_barrier(jnp.sum(exp_old, axis=1)) + exp_new
        probs_old = (exp_old / denom[:, None]).astype(jnp.bfloat16)
        probs_new = (exp_new / denom).astype(jnp.bfloat16)
        mixed = jnp.einsum('hp,pc->hc', probs_old.astype(jnp.float32), cache_f[:, :KVL])
        mixed = mixed + probs_new.astype(jnp.float32)[:, None] * entry_f[None, :KVL]
        return mixed.astype(jnp.bfloat16)
    attn_out = lax.map(attend, (queries, cache, new_entry, lengths))
    return (hidden, new_entry, attn_out)
```

```python
import jax
import jax.numpy as jnp
from jax import lax
from jax.sharding import PartitionSpec as P

KVL = 512
EXPERTS = 16
AXES = ("sec", "dev")
SIDE = 4
STRIDE = {"x": 16, "y": 4, "z": 1}
SLOT_ORDER = ((("x", "y", "z"), ("y", "z", "x")), (("z", "x", "y"), ("z", "x", "y")))
LANES = 128
GATHER_CUT = 38 * LANES
SCATTER_CUT = 38 * LANES


norm_eps = 1e-06
SCORE_SCALE = 0.0721687836


def rms_scale(values, gain_vec):
    values = values.astype(jnp.float32)
    return (
        values * lax.rsqrt(jnp.mean(values * values, axis=-1, keepdims=True) + norm_eps) * gain_vec
    )


def rotate_half(rotary, positions):
    half_dim = rotary.shape[-1] // 2
    inv_freq = jnp.exp(
        -jnp.log(10000.0) * jnp.arange(half_dim).astype(jnp.float32) * 2.0 / rotary.shape[-1]
    )
    angles = positions.astype(jnp.float32)[:, None] * inv_freq[None, :]
    lower_half = rotary[:, :half_dim]
    upper_half = rotary[:, half_dim:]
    cosine = jnp.cos(angles)
    sine_val = jnp.sin(angles)
    return jnp.concatenate(
        [lower_half * cosine - upper_half * sine_val, upper_half * cosine + lower_half * sine_val],
        axis=-1,
    )


def shift_pairs(slot, phase, amount):
    pairs = []
    for sec in range(2):
        stride = STRIDE[SLOT_ORDER[slot][sec][phase]]
        for dev in range(SIDE**3):
            place = dev // stride % SIDE
            there = dev + ((place + amount) % SIDE - place) * stride
            pairs.append((sec * SIDE**3 + dev, sec * SIDE**3 + there))
    return pairs


def gather_phase(block, slot, phase):
    return [block] + [
        lax.ppermute(block, AXES, shift_pairs(slot, phase, back)) for back in range(1, SIDE)
    ]


def scatter_phase(parts, slot, phase):
    total = parts[0].astype(jnp.float32)
    for back in range(1, SIDE):
        total = total + lax.ppermute(
            parts[back], AXES, shift_pairs(slot, phase, -back)
        ).astype(jnp.float32)
    return total


def on_device(
    resid,
    ffn_gain,
    expert_ids,
    gate_weights,
    w_gate,
    w_up,
    w_down,
    attn_gain,
    w_kv,
    kv_gain,
    cache,
    lengths,
    queries,
):
    tok_count = resid.shape[0]
    model_width = resid.shape[1]
    sec = lax.axis_index("sec")
    chip_expert = lax.axis_index("dev") // (SIDE**3 // (EXPERTS // 2))
    gate_pair = lax.all_gather(w_gate, "sec", axis=0, tiled=False)
    up_pair = lax.all_gather(w_up, "sec", axis=0, tiled=False)
    down_pair = lax.all_gather(w_down, "sec", axis=0, tiled=True)

    normed = rms_scale(resid, ffn_gain).astype(jnp.bfloat16)
    dense_weights = jnp.sum(
        jnp.where(
            expert_ids[:, :, None] == jnp.arange(EXPERTS, dtype=jnp.int32)[None, None, :],
            gate_weights[:, :, None],
            0.0,
        ),
        axis=1,
    )
    high = dense_weights.astype(jnp.bfloat16)
    rest = dense_weights - high.astype(jnp.float32)
    middle = rest.astype(jnp.bfloat16)
    low = (rest - middle.astype(jnp.float32)).astype(jnp.bfloat16)
    weight_cols = jnp.concatenate(
        [high, middle, low, jnp.zeros((tok_count, LANES - 3 * EXPERTS), jnp.bfloat16)], axis=1
    )
    rows = [normed[:, :GATHER_CUT], jnp.concatenate([normed[:, GATHER_CUT:], weight_cols], axis=1)]
    for phase in range(3):
        parts = [gather_phase(rows[slot], slot, phase) for slot in range(2)]
        rows = [jnp.concatenate(part, axis=0) for part in parts]

    def to_first(values):
        wide = values.reshape(SIDE, SIDE, SIDE, tok_count, values.shape[-1])
        return jnp.where(
            sec == 0, wide.transpose(2, 0, 1, 3, 4), wide.transpose(1, 2, 0, 3, 4)
        ).reshape(values.shape)

    def to_second(values):
        wide = values.reshape(SIDE, SIDE, SIDE, tok_count, values.shape[-1])
        return jnp.where(
            sec == 0, wide.transpose(1, 2, 0, 3, 4), wide.transpose(2, 0, 1, 3, 4)
        ).reshape(values.shape)

    feature_rest = model_width - GATHER_CUT
    acts = []
    for pair in (gate_pair, up_pair):
        first = jnp.einsum(
            "td,sdf->tsf", rows[0], pair[:, :GATHER_CUT], preferred_element_type=jnp.float32
        )
        second = jnp.einsum(
            "td,sdf->tsf",
            rows[1][:, :feature_rest],
            pair[:, GATHER_CUT:],
            preferred_element_type=jnp.float32,
        )
        second = to_first(second.reshape(second.shape[0], -1)).reshape(second.shape)
        acts.append(first + second)
    cols = to_first(rows[1][:, feature_rest:].astype(jnp.float32))
    dense = cols[:, :EXPERTS] + cols[:, EXPERTS : 2 * EXPERTS]
    dense = dense + cols[:, 2 * EXPERTS : 3 * EXPERTS]
    mine = jnp.arange(EXPERTS, dtype=jnp.int32)[None, :] == (
        chip_expert + jnp.arange(2, dtype=jnp.int32)[:, None] * (EXPERTS // 2)
    )
    weight_pair = jnp.sum(jnp.where(mine[None], dense[:, None, :], 0.0), axis=-1)
    hidden_act = jax.nn.silu(acts[0]) * acts[1] * weight_pair[:, :, None]
    hidden_act = hidden_act.astype(jnp.bfloat16).reshape(hidden_act.shape[0], -1)
    sums = []
    for slot in range(2):
        left = hidden_act if slot == 0 else to_second(hidden_act)
        right = down_pair[:, :SCATTER_CUT] if slot == 0 else down_pair[:, SCATTER_CUT:]
        total = jnp.dot(left, right, preferred_element_type=jnp.float32)
        for phase in (2, 1, 0):
            wide = total.astype(jnp.bfloat16)
            parts = jnp.split(wide, SIDE, axis=0)
            total = scatter_phase(parts, slot, phase)
        sums.append(total)
    moe = jnp.concatenate(sums, axis=1)
    hidden = (resid.astype(jnp.float32) + moe).astype(jnp.bfloat16)
    attn_in = rms_scale(hidden, attn_gain).astype(jnp.bfloat16)
    kv_raw = jnp.dot(attn_in, w_kv, preferred_element_type=jnp.float32)
    latent = rms_scale(kv_raw[:, :KVL], kv_gain)
    rotated = rotate_half(kv_raw[:, KVL:], lengths)
    new_entry = jnp.concatenate([latent, rotated], axis=-1).astype(jnp.bfloat16)
    scores_old = (
        jnp.einsum("thc,tpc->thp", queries, cache, preferred_element_type=jnp.float32) * SCORE_SCALE
    )
    scores_new = (
        jnp.einsum("thc,tc->th", queries, new_entry, preferred_element_type=jnp.float32)
        * SCORE_SCALE
    )
    live_mask = jnp.arange(cache.shape[1], dtype=jnp.int32)[None, None, :] < lengths[:, None, None]
    scores_old = jnp.where(live_mask, scores_old, -jnp.inf)
    peak = jnp.maximum(jnp.max(scores_old, axis=2), scores_new)
    exp_old = jnp.exp(scores_old - peak[:, :, None])
    exp_new = jnp.exp(scores_new - peak)
    denom = jnp.sum(exp_old, axis=2) + exp_new
    probs_old = (exp_old / denom[:, :, None]).astype(jnp.bfloat16)
    probs_new = (exp_new / denom).astype(jnp.bfloat16)
    mixed = jnp.einsum(
        "thp,tpc->thc", probs_old, cache[:, :, :KVL], preferred_element_type=jnp.float32
    )
    mixed = mixed + probs_new.astype(jnp.float32)[:, :, None] * new_entry[:, None, :KVL].astype(
        jnp.float32
    )
    attn_out = mixed.astype(jnp.bfloat16)
    return (hidden, new_entry, attn_out)


def solution(mesh):
    placed = (
        P(("sec", "dev"), None),
        P(),
        P(("sec", "dev"), None),
        P(("sec", "dev"), None),
        P(None, ("sec", "dev")),
        P(None, ("sec", "dev")),
        P(("sec", "dev"), None),
        P(),
        P(),
        P(),
        P(("sec", "dev"), None, None),
        P(("sec", "dev")),
        P(("sec", "dev"), None, None),
    )
    return jax.shard_map(
        on_device,
        mesh=mesh,
        in_specs=placed,
        out_specs=(P(("sec", "dev"), None), P(("sec", "dev"), None), P(("sec", "dev"), None, None)),
        check_vma=False,
    )
```

```python
import jax
import jax.numpy as jnp
from jax import lax
from jax.experimental import pallas as pl
from jax.experimental.pallas import tpu as pltpu
from jax.sharding import PartitionSpec as P

KVL = 512
EXPERTS = 16
AXES = ("sec", "dev")
SIDE = 4
STRIDE = {"x": 16, "y": 4, "z": 1}
SLOT_ORDER = ((("x", "y", "z"), ("y", "z", "x")), (("z", "x", "y"), ("z", "x", "y")))
LANES = 128
GATHER_CUT = 38 * LANES
SCATTER_CUT = 38 * LANES


norm_eps = 1e-06
SCORE_SCALE = 0.0721687836


def rms_scale(values, gain_vec):
    values = values.astype(jnp.float32)
    return (
        values * lax.rsqrt(jnp.mean(values * values, axis=-1, keepdims=True) + norm_eps) * gain_vec
    )


def rotate_half(rotary, positions):
    half_dim = rotary.shape[-1] // 2
    inv_freq = jnp.exp(
        -jnp.log(10000.0) * jnp.arange(half_dim).astype(jnp.float32) * 2.0 / rotary.shape[-1]
    )
    angles = positions.astype(jnp.float32)[:, None] * inv_freq[None, :]
    lower_half = rotary[:, :half_dim]
    upper_half = rotary[:, half_dim:]
    cosine = jnp.cos(angles)
    sine_val = jnp.sin(angles)
    return jnp.concatenate(
        [lower_half * cosine - upper_half * sine_val, upper_half * cosine + lower_half * sine_val],
        axis=-1,
    )


def shift_pairs(slot, phase, amount):
    pairs = []
    for sec in range(2):
        stride = STRIDE[SLOT_ORDER[slot][sec][phase]]
        for dev in range(SIDE**3):
            place = dev // stride % SIDE
            there = dev + ((place + amount) % SIDE - place) * stride
            pairs.append((sec * SIDE**3 + dev, sec * SIDE**3 + there))
    return pairs


def swap_cores(values):
    return lax.ppermute(values, AXES, [(i, (i + SIDE**3) % (2 * SIDE**3)) for i in range(2 * SIDE**3)])


def after(values, *earlier):
    return lax.optimization_barrier((values, *earlier))[0]


def exchange(blocks, phase, sign):
    got = [[blocks[slot][0]] + [None] * (SIDE - 1) for slot in range(2)]
    for slot in range(2):
        for back in (1, 3, 2):
            got[slot][back] = lax.ppermute(
                blocks[slot][back], AXES, shift_pairs(slot, phase, sign * back)
            )
    return got


def gather_last(rows):
    near = [
        [lax.ppermute(rows[slot], AXES, shift_pairs(slot, 2, way)) for way in (1, -1)]
        for slot in range(2)
    ]
    near = lax.optimization_barrier(near)
    half = rows[0].shape[0] // 2
    far = [
        [
            lax.ppermute(near[slot][0][:half], AXES, shift_pairs(slot, 2, 1)),
            lax.ppermute(near[slot][1][half:], AXES, shift_pairs(slot, 2, -1)),
        ]
        for slot in range(2)
    ]
    return [
        [rows[slot], near[slot][0], far[slot][0], far[slot][1], near[slot][1]] for slot in range(2)
    ]


def scatter_first(parts):
    half = parts[0][0].shape[0] // 2
    far = [
        [
            lax.ppermute(parts[slot][2][:half], AXES, shift_pairs(slot, 2, -1)),
            lax.ppermute(parts[slot][2][half:], AXES, shift_pairs(slot, 2, 1)),
        ]
        for slot in range(2)
    ]

    def plus(one, two):
        return one.astype(jnp.float32) + two.astype(jnp.float32)

    joined = []
    for slot in range(2):
        back = plus(parts[slot][1][:half], far[slot][0]).astype(jnp.bfloat16)
        ahead = plus(parts[slot][3][half:], far[slot][1]).astype(jnp.bfloat16)
        joined.append(
            [
                jnp.concatenate([back, parts[slot][1][half:]], axis=0),
                jnp.concatenate([parts[slot][3][:half], ahead], axis=0),
            ]
        )
    joined = lax.optimization_barrier(joined)
    return [
        plus(parts[slot][0], lax.ppermute(joined[slot][0], AXES, shift_pairs(slot, 2, -1)))
        + lax.ppermute(joined[slot][1], AXES, shift_pairs(slot, 2, 1)).astype(jnp.float32)
        for slot in range(2)
    ]


def join_body(*refs):
    ins, outs, sems = refs[: 2 * SIDE], refs[2 * SIDE : 2 * SIDE + 2], refs[-1]
    copies = []
    for slot in range(2):
        for back in range(SIDE):
            source = ins[slot * SIDE + back]
            count = source.shape[0]
            copies.append(
                pltpu.make_async_copy(
                    source,
                    outs[slot].at[pl.ds(back * count, count)],
                    sems.at[slot * SIDE + back],
                )
            )
    for copy in copies:
        copy.start()
    for copy in copies:
        copy.wait()


def join(got):
    shapes = [
        jax.ShapeDtypeStruct((SIDE * part[0].shape[0], *part[0].shape[1:]), part[0].dtype)
        for part in got
    ]
    return pl.pallas_call(
        join_body,
        out_shape=shapes,
        in_specs=[pl.BlockSpec(memory_space=pl.ANY)] * (2 * SIDE),
        out_specs=[pl.BlockSpec(memory_space=pl.ANY)] * 2,
        scratch_shapes=[pltpu.SemaphoreType.DMA((2 * SIDE,))],
        compiler_params=pltpu.CompilerParams(vmem_limit_bytes=1 << 20),
        name="join",
    )(*got[0], *got[1])


CHUNKS = ((1, 0, 8), (1, 8, 18), (0, 0, 12), (0, 12, 24), (0, 24, 38))


PIECES = 5


def act_body(info_ref, *refs):
    rows = (refs[0:PIECES], refs[PIECES : 2 * PIECES])
    weights = refs[2 * PIECES : 2 * PIECES + 4]
    first_out, second_out = refs[2 * PIECES + 4 : 2 * PIECES + 6]
    x_first, x_second, w_all, acc_first, acc_second, scale, sems = refs[2 * PIECES + 6 :]
    held = (x_first, x_second)
    accs = (acc_first, acc_second)
    wide = weights[0].shape[1]
    plans = []
    for number, (slot, low, high) in enumerate(CHUNKS):
        ends = high * LANES
        if slot == 1 and high == CHUNKS[1][2]:
            ends += LANES
        base = slot * GATHER_CUT
        copies = []
        start = 0
        for piece in range(PIECES):
            group = rows[slot][piece].shape[0]
            copies.append(
                pltpu.make_async_copy(
                    rows[slot][piece].at[:, pl.ds(low * LANES, ends - low * LANES)],
                    held[slot].at[pl.ds(start, group), pl.ds(low * LANES, ends - low * LANES)],
                    sems.at[number, piece],
                )
            )
            start += group
        for which in range(4):
            span = pl.ds(base + low * LANES, (high - low) * LANES)
            copies.append(
                pltpu.make_async_copy(
                    weights[which].at[span, :],
                    w_all.at[span, pl.ds(which * wide, wide)],
                    sems.at[number, PIECES + which],
                )
            )
        plans.append(copies)
        for copy in copies:
            copy.start()
    seen = set()
    for number, (slot, low, high) in enumerate(CHUNKS):
        for copy in plans[number]:
            copy.wait()
        new = slot not in seen
        seen.add(slot)

        def column(which, carry, slot=slot, low=low, high=high, new=new):
            at = pl.ds(pl.multiple_of(which * wide, wide), wide)
            part = jnp.dot(
                held[slot][:, low * LANES : high * LANES],
                w_all[slot * GATHER_CUT + low * LANES : slot * GATHER_CUT + high * LANES, at],
                preferred_element_type=jnp.float32,
            )
            accs[slot][:, at] = part if new else accs[slot][:, at] + part
            return carry

        lax.fori_loop(0, 4, column, 0)
    features = CHUNKS[1][2] * LANES
    cols = x_second[:, features : features + LANES].astype(jnp.float32)
    lane = lax.broadcasted_iota(jnp.int32, (1, LANES), 1)
    for which in range(2):
        expert = info_ref[3 + which]
        hit = (lane == expert) | (lane == expert + EXPERTS) | (lane == expert + 2 * EXPERTS)
        value = jnp.sum(jnp.where(hit, cols, 0.0), axis=1, keepdims=True)
        scale[:, which * LANES : (which + 1) * LANES] = jnp.broadcast_to(
            value, (cols.shape[0], LANES)
        )

    def finish(pair, carry):
        outer, middle = pair // SIDE, pair % SIDE
        for inner in range(SIDE):
            there = outer * info_ref[0] + middle * info_ref[1] + inner * info_ref[2]
            mine = pl.ds(pl.multiple_of(pair * (SIDE * 8) + inner * 8, 8), 8)
            other = pl.ds(pl.multiple_of(there * 8, 8), 8)
            for which in range(2):
                low = which * wide
                gate = acc_first[mine, low : low + wide] + acc_second[other, low : low + wide]
                low = (2 + which) * wide
                up = acc_first[mine, low : low + wide] + acc_second[other, low : low + wide]
                weight = scale[other, which * LANES : (which + 1) * LANES]
                weight = jnp.concatenate([weight] * (wide // LANES), axis=1)
                act = (gate / (1.0 + jnp.exp(-gate)) * up * weight).astype(jnp.bfloat16)
                first_out[pair * SIDE + inner, :, which * wide : (which + 1) * wide] = act
                second_out[there, :, which * wide : (which + 1) * wide] = act
        return carry

    lax.fori_loop(0, SIDE * SIDE, finish, 0)


def expert_acts(info, first_rows, second_rows, weights):
    tokens = sum(part.shape[0] for part in first_rows)
    wide = weights[0].shape[1]
    out = jax.ShapeDtypeStruct((tokens // 8, 8, 2 * wide), jnp.bfloat16)
    hbm = pl.BlockSpec(memory_space=pl.ANY)
    first, second = pl.pallas_call(
        act_body,
        out_shape=[out, out],
        in_specs=[pl.BlockSpec(memory_space=pltpu.SMEM)]
        + [pl.BlockSpec(memory_space=pltpu.VMEM)] * (2 * PIECES)
        + [hbm] * 4,
        out_specs=[pl.BlockSpec(memory_space=pltpu.VMEM)] * 2,
        scratch_shapes=[
            pltpu.VMEM((tokens, first_rows[0].shape[1]), jnp.bfloat16),
            pltpu.VMEM((tokens, second_rows[0].shape[1]), jnp.bfloat16),
            pltpu.VMEM((weights[0].shape[0], 4 * wide), jnp.bfloat16),
            pltpu.VMEM((tokens, 4 * wide), jnp.float32),
            pltpu.VMEM((tokens, 4 * wide), jnp.float32),
            pltpu.VMEM((tokens, 2 * LANES), jnp.float32),
            pltpu.SemaphoreType.DMA((len(CHUNKS), PIECES + 4)),
        ],
        compiler_params=pltpu.CompilerParams(vmem_limit_bytes=34 << 20),
        cost_estimate=pl.CostEstimate(
            flops=8 * tokens * weights[0].shape[0] * wide, bytes_accessed=24 << 20, transcendentals=0
        ),
        name="expert_acts",
    )(info, *first_rows, *second_rows, *weights)
    return first.reshape(tokens, 2 * wide), second.reshape(tokens, 2 * wide)


def down_body(acts_ref, mine_ref, other_ref, *outs):
    wide = mine_ref.shape[0]
    group = acts_ref.shape[0] // SIDE
    step = 2 * LANES
    total = outs[0].shape[1]
    for low in range(0, total, step):
        high = min(low + step, total)
        part = jnp.dot(
            acts_ref[:, :wide], mine_ref[:, low:high], preferred_element_type=jnp.float32
        ) + jnp.dot(acts_ref[:, wide:], other_ref[:, low:high], preferred_element_type=jnp.float32)
        part = part.astype(jnp.bfloat16)
        for back in range(SIDE):
            outs[back][:, low:high] = part[back * group : (back + 1) * group]


def expert_outs(acts, mine, other, first_block, steps, block):
    tokens, both = acts.shape
    group = tokens // SIDE
    spec = pl.BlockSpec((both // 2, SCATTER_CUT // 2), lambda i: (0, i + first_block))
    return pl.pallas_call(
        down_body,
        grid=(steps,),
        out_shape=[jax.ShapeDtypeStruct((group, steps * block), jnp.bfloat16)] * SIDE,
        in_specs=[pl.BlockSpec((tokens, both), lambda i: (0, 0)), spec, spec],
        out_specs=[pl.BlockSpec((group, block), lambda i: (0, i))] * SIDE,
        compiler_params=pltpu.CompilerParams(vmem_limit_bytes=16 << 20),
        cost_estimate=pl.CostEstimate(
            flops=2 * tokens * both * steps * block,
            bytes_accessed=2 * (tokens + both) * steps * block,
            transcendentals=0,
        ),
        name="expert_outs",
    )(acts, mine, other)


def on_device(
    resid,
    ffn_gain,
    expert_ids,
    gate_weights,
    w_gate,
    w_up,
    w_down,
    attn_gain,
    w_kv,
    kv_gain,
    cache,
    lengths,
    queries,
):
    tok_count = resid.shape[0]
    model_width = resid.shape[1]
    sec = lax.axis_index("sec")
    chip_expert = lax.axis_index("dev") // (SIDE**3 // (EXPERTS // 2))
    gate_other = swap_cores(w_gate)
    normed = rms_scale(resid, ffn_gain).astype(jnp.bfloat16)
    dense_weights = jnp.sum(
        jnp.where(
            expert_ids[:, :, None] == jnp.arange(EXPERTS, dtype=jnp.int32)[None, None, :],
            gate_weights[:, :, None],
            0.0,
        ),
        axis=1,
    )
    high = dense_weights.astype(jnp.bfloat16)
    rest = dense_weights - high.astype(jnp.float32)
    middle = rest.astype(jnp.bfloat16)
    low = (rest - middle.astype(jnp.float32)).astype(jnp.bfloat16)
    weight_cols = jnp.concatenate(
        [high, middle, low, jnp.zeros((tok_count, LANES - 3 * EXPERTS), jnp.bfloat16)], axis=1
    )
    rows = [normed[:, :GATHER_CUT], jnp.concatenate([normed[:, GATHER_CUT:], weight_cols], axis=1)]
    rows = [part[None] for part in rows]
    got = exchange([[part] * SIDE for part in rows], 0, 1)
    rows = join(lax.optimization_barrier((got, gate_other))[0])
    up_other = swap_cores(after(w_up, *rows))
    got = exchange([[part] * SIDE for part in rows], 1, 1)
    rows = join(lax.optimization_barrier((got, up_other))[0])
    down_other = swap_cores(after(w_down, *rows))
    got = gather_last(rows)
    got = [[part.reshape(-1, part.shape[-1]) for part in parts] for parts in got]
    strides = jnp.where(
        sec == 0, jnp.array([1, 16, 4], jnp.int32), jnp.array([4, 1, 16], jnp.int32)
    )
    half = EXPERTS // 2
    experts = jnp.stack([chip_expert + sec * half, chip_expert + (1 - sec) * half])
    info = jnp.concatenate([strides, experts.astype(jnp.int32)])
    acts = expert_acts(info, got[0], got[1], (w_gate, gate_other, w_up, up_other))
    first = expert_outs(acts[0], w_down, down_other, 0, 2, SCATTER_CUT // 2)
    second = expert_outs(acts[1], w_down, down_other, 2, 1, model_width - SCATTER_CUT)
    parts = lax.optimization_barrier([list(first), list(second)])
    for phase in (2, 1, 0):
        if phase == 2:
            sums = scatter_first(parts)
        else:
            got = exchange(parts, phase, -1)
            sums = []
            for slot in range(2):
                total = got[slot][0].astype(jnp.float32)
                for back in range(1, SIDE):
                    total = total + got[slot][back].astype(jnp.float32)
                sums.append(total)
        if phase > 0:
            sums = lax.optimization_barrier([total.astype(jnp.bfloat16) for total in sums])
            parts = [jnp.split(total, SIDE, axis=0) for total in sums]
    moe = jnp.concatenate(sums, axis=1)
    hidden = (resid.astype(jnp.float32) + moe).astype(jnp.bfloat16)
    attn_in = rms_scale(hidden, attn_gain).astype(jnp.bfloat16)
    kv_raw = jnp.dot(attn_in, w_kv, preferred_element_type=jnp.float32)
    latent = rms_scale(kv_raw[:, :KVL], kv_gain)
    rotated = rotate_half(kv_raw[:, KVL:], lengths)
    new_entry = jnp.concatenate([latent, rotated], axis=-1).astype(jnp.bfloat16)
    scores_old = (
        jnp.einsum("thc,tpc->thp", queries, cache, preferred_element_type=jnp.float32) * SCORE_SCALE
    )
    scores_new = (
        jnp.einsum("thc,tc->th", queries, new_entry, preferred_element_type=jnp.float32)
        * SCORE_SCALE
    )
    live_mask = jnp.arange(cache.shape[1], dtype=jnp.int32)[None, None, :] < lengths[:, None, None]
    scores_old = jnp.where(live_mask, scores_old, -jnp.inf)
    peak = jnp.maximum(jnp.max(scores_old, axis=2), scores_new)
    exp_old = jnp.exp(scores_old - peak[:, :, None])
    exp_new = jnp.exp(scores_new - peak)
    denom = jnp.sum(exp_old, axis=2) + exp_new
    probs_old = (exp_old / denom[:, :, None]).astype(jnp.bfloat16)
    probs_new = (exp_new / denom).astype(jnp.bfloat16)
    mixed = jnp.einsum(
        "thp,tpc->thc", probs_old, cache[:, :, :KVL], preferred_element_type=jnp.float32
    )
    mixed = mixed + probs_new.astype(jnp.float32)[:, :, None] * new_entry[:, None, :KVL].astype(
        jnp.float32
    )
    attn_out = mixed.astype(jnp.bfloat16)
    return (hidden, new_entry, attn_out)


def solution(mesh):
    placed = (
        P(("sec", "dev"), None),
        P(),
        P(("sec", "dev"), None),
        P(("sec", "dev"), None),
        P(None, ("sec", "dev")),
        P(None, ("sec", "dev")),
        P(("sec", "dev"), None),
        P(),
        P(),
        P(),
        P(("sec", "dev"), None, None),
        P(("sec", "dev")),
        P(("sec", "dev"), None, None),
    )
    return jax.shard_map(
        on_device,
        mesh=mesh,
        in_specs=placed,
        out_specs=(P(("sec", "dev"), None), P(("sec", "dev"), None), P(("sec", "dev"), None, None)),
        check_vma=False,
    )
```

```python
import functools

import jax
import jax.numpy as jnp
from jax import lax
from jax.experimental import pallas as pl
from jax.experimental.pallas import tpu as pltpu
from jax.sharding import PartitionSpec as P

KVL = 512
EXPERTS = 16
AXES = ("sec", "dev")
SIDE = 4
STRIDE = {"x": 16, "y": 4, "z": 1}
ORDER = (("x", "y", "z"), ("y", "z", "x"))
LANES = 128


norm_eps = 1e-06
SCORE_SCALE = 0.0721687836


def rms_scale(values, gain_vec):
    values = values.astype(jnp.float32)
    return (
        values * lax.rsqrt(jnp.mean(values * values, axis=-1, keepdims=True) + norm_eps) * gain_vec
    )


def rotate_half(rotary, positions):
    half_dim = rotary.shape[-1] // 2
    inv_freq = jnp.exp(
        -jnp.log(10000.0) * jnp.arange(half_dim).astype(jnp.float32) * 2.0 / rotary.shape[-1]
    )
    angles = positions.astype(jnp.float32)[:, None] * inv_freq[None, :]
    lower_half = rotary[:, :half_dim]
    upper_half = rotary[:, half_dim:]
    cosine = jnp.cos(angles)
    sine_val = jnp.sin(angles)
    return jnp.concatenate(
        [lower_half * cosine - upper_half * sine_val, upper_half * cosine + lower_half * sine_val],
        axis=-1,
    )


def shift(values, phase, amount):
    pairs = []
    for sec in range(2):
        stride = STRIDE[ORDER[sec][phase]]
        for dev in range(SIDE**3):
            place = dev // stride % SIDE
            there = dev + ((place + amount) % SIDE - place) * stride
            pairs.append((sec * SIDE**3 + dev, sec * SIDE**3 + there))
    return lax.ppermute(values, AXES, pairs)


def swap_cores(values):
    return lax.ppermute(values, AXES, [(i, (i + SIDE**3) % (2 * SIDE**3)) for i in range(2 * SIDE**3)])


def after(values, *earlier):
    return lax.optimization_barrier((values, *earlier))[0]


def join_body(count, *refs):
    ins, outs, sems = refs[:SIDE], refs[SIDE : SIDE + count], refs[-1]
    each = SIDE // count
    copies = []
    for back in range(SIDE):
        rows = ins[back].shape[0]
        copies.append(
            pltpu.make_async_copy(
                ins[back],
                outs[back // each].at[pl.ds(back % each * rows, rows)],
                sems.at[back],
            )
        )
    for copy in copies:
        copy.start()
    for copy in copies:
        copy.wait()


def join(blocks, count):
    rows, *rest = blocks[0].shape
    hbm = pl.BlockSpec(memory_space=pl.ANY)
    return pl.pallas_call(
        functools.partial(join_body, count),
        out_shape=[jax.ShapeDtypeStruct((SIDE // count * rows, *rest), blocks[0].dtype)] * count,
        in_specs=[hbm] * SIDE,
        out_specs=[hbm] * count,
        scratch_shapes=[pltpu.SemaphoreType.DMA((SIDE,))],
        compiler_params=pltpu.CompilerParams(vmem_limit_bytes=1 << 20),
        name="join",
    )(*blocks)


def act_body(info_ref, *refs):
    rows, weights, out_ref = refs[:SIDE], refs[SIDE : 2 * SIDE], refs[2 * SIDE]
    depth, wide = weights[0].shape
    held = jnp.concatenate([part[:, depth:] for part in rows], axis=0).astype(jnp.float32)
    lane = lax.broadcasted_iota(jnp.int32, (1, LANES), 1)

    def product(which):
        left = jnp.concatenate([part[:, :depth] for part in rows], axis=0)
        return jnp.dot(left, weights[which][...], preferred_element_type=jnp.float32)

    for which in range(2):
        expert = info_ref[which]
        hit = (lane == expert) | (lane == expert + EXPERTS) | (lane == expert + 2 * EXPERTS)
        weight = jnp.sum(jnp.where(hit, held, 0.0), axis=1, keepdims=True)
        gate = product(which)
        up = product(2 + which)
        act = gate / (1.0 + jnp.exp(-gate)) * up * weight
        out_ref[:, which * wide : (which + 1) * wide] = act.astype(jnp.bfloat16)


def expert_acts(info, rows, weights):
    tokens = SIDE * rows[0].shape[0]
    depth, wide = weights[0].shape
    vmem = pl.BlockSpec(memory_space=pltpu.VMEM)
    return pl.pallas_call(
        act_body,
        out_shape=jax.ShapeDtypeStruct((tokens, 2 * wide), jnp.bfloat16),
        in_specs=[pl.BlockSpec(memory_space=pltpu.SMEM)] + [vmem] * (2 * SIDE),
        out_specs=vmem,
        compiler_params=pltpu.CompilerParams(vmem_limit_bytes=30 << 20),
        cost_estimate=pl.CostEstimate(
            flops=8 * tokens * depth * wide, bytes_accessed=1 << 20, transcendentals=0
        ),
        name="expert_acts",
    )(info, *rows, *weights)


def down_body(acts_ref, mine_ref, other_ref, *outs):
    wide = mine_ref.shape[0]
    group = acts_ref.shape[0] // SIDE
    step = 2 * LANES
    for low in range(0, mine_ref.shape[1], step):
        high = low + step
        part = jnp.dot(
            acts_ref[:, :wide], mine_ref[:, low:high], preferred_element_type=jnp.float32
        ) + jnp.dot(acts_ref[:, wide:], other_ref[:, low:high], preferred_element_type=jnp.float32)
        part = part.astype(jnp.bfloat16)
        for back in range(SIDE):
            outs[back][:, low:high] = part[back * group : (back + 1) * group]


def expert_outs(acts, mine, other):
    tokens, both = acts.shape
    group, width, steps = tokens // SIDE, mine.shape[1], 4
    block = width // steps
    spec = pl.BlockSpec((both // 2, block), lambda i: (0, i))
    return pl.pallas_call(
        down_body,
        grid=(steps,),
        out_shape=[jax.ShapeDtypeStruct((group, width), jnp.bfloat16)] * SIDE,
        in_specs=[pl.BlockSpec((tokens, both), lambda i: (0, 0)), spec, spec],
        out_specs=[pl.BlockSpec((group, block), lambda i: (0, i))] * SIDE,
        compiler_params=pltpu.CompilerParams(vmem_limit_bytes=12 << 20),
        cost_estimate=pl.CostEstimate(
            flops=2 * tokens * both * width, bytes_accessed=1 << 20, transcendentals=0
        ),
        name="expert_outs",
    )(acts, mine, other)


def plus(first, *others):
    total = first.astype(jnp.float32)
    for other in others:
        total = total + other.astype(jnp.float32)
    return total


def on_device(
    resid,
    ffn_gain,
    expert_ids,
    gate_weights,
    w_gate,
    w_up,
    w_down,
    attn_gain,
    w_kv,
    kv_gain,
    cache,
    lengths,
    queries,
):
    tok_count = resid.shape[0]
    model_width = resid.shape[1]
    sec = lax.axis_index("sec")
    chip_expert = lax.axis_index("dev") // (SIDE**3 // (EXPERTS // 2))
    gate_other = swap_cores(w_gate)
    normed = rms_scale(resid, ffn_gain).astype(jnp.bfloat16)
    dense_weights = jnp.sum(
        jnp.where(
            expert_ids[:, :, None] == jnp.arange(EXPERTS, dtype=jnp.int32)[None, None, :],
            gate_weights[:, :, None],
            0.0,
        ),
        axis=1,
    )
    high = dense_weights.astype(jnp.bfloat16)
    rest = dense_weights - high.astype(jnp.float32)
    middle = rest.astype(jnp.bfloat16)
    low = (rest - middle.astype(jnp.float32)).astype(jnp.bfloat16)
    weight_cols = jnp.concatenate(
        [high, middle, low, jnp.zeros((tok_count, LANES - 3 * EXPERTS), jnp.bfloat16)], axis=1
    )
    rows = jnp.concatenate([normed, weight_cols], axis=1)[None]
    got = [rows] + [shift(rows, 0, back) for back in range(1, SIDE)]
    (rows,) = join(lax.optimization_barrier((got, gate_other))[0], 1)
    up_other = swap_cores(after(w_up, rows))
    got = [rows] + [shift(rows, 1, back) for back in range(1, SIDE)]
    low, high = join(lax.optimization_barrier((got, up_other))[0], 2)
    down_other = swap_cores(after(w_down, low))
    low_back, high_ahead = shift(low, 2, 1), shift(high, 2, -1)
    high_back, low_ahead = shift(high, 2, 1), shift(low, 2, -1)
    low_far, high_far = shift(low_back, 2, 1), shift(high_ahead, 2, -1)

    half = EXPERTS // 2
    info = jnp.stack([chip_expert + sec * half, chip_expert + (1 - sec) * half]).astype(jnp.int32)
    weights = (w_gate, gate_other, w_up, up_other)

    def flat(*parts):
        return [part.reshape(-1, part.shape[-1]) for part in parts]

    acts = expert_acts(info, flat(low, high, low_back, high_ahead), weights)
    low_mine, high_mine, low_back, high_ahead = expert_outs(acts, w_down, down_other)
    info = after(info, low_mine)
    acts = expert_acts(info, flat(high_back, low_ahead, low_far, high_far), weights)
    high_back, low_ahead, low_far, high_far = expert_outs(acts, w_down, down_other)

    low_far, high_far = shift(low_far, 2, -1), shift(high_far, 2, 1)
    high_back, low_ahead = shift(high_back, 2, -1), shift(low_ahead, 2, 1)
    low_back = shift(plus(low_back, low_far).astype(jnp.bfloat16), 2, -1)
    high_ahead = shift(plus(high_ahead, high_far).astype(jnp.bfloat16), 2, 1)
    low = plus(low_mine, low_back, low_ahead).astype(jnp.bfloat16)
    high = plus(high_mine, high_back, high_ahead).astype(jnp.bfloat16)
    parts = [*jnp.split(low, 2, axis=0), *jnp.split(high, 2, axis=0)]
    for phase in (1, 0):
        moe = plus(parts[0], *(shift(parts[back], phase, -back) for back in range(1, SIDE)))
        if phase > 0:
            parts = jnp.split(moe.astype(jnp.bfloat16), SIDE, axis=0)
    hidden = (resid.astype(jnp.float32) + moe).astype(jnp.bfloat16)
    attn_in = rms_scale(hidden, attn_gain).astype(jnp.bfloat16)
    kv_raw = jnp.dot(attn_in, w_kv, preferred_element_type=jnp.float32)
    latent = rms_scale(kv_raw[:, :KVL], kv_gain)
    rotated = rotate_half(kv_raw[:, KVL:], lengths)
    new_entry = jnp.concatenate([latent, rotated], axis=-1).astype(jnp.bfloat16)
    scores_old = (
        jnp.einsum("thc,tpc->thp", queries, cache, preferred_element_type=jnp.float32) * SCORE_SCALE
    )
    scores_new = (
        jnp.einsum("thc,tc->th", queries, new_entry, preferred_element_type=jnp.float32)
        * SCORE_SCALE
    )
    live_mask = jnp.arange(cache.shape[1], dtype=jnp.int32)[None, None, :] < lengths[:, None, None]
    scores_old = jnp.where(live_mask, scores_old, -jnp.inf)
    peak = jnp.maximum(jnp.max(scores_old, axis=2), scores_new)
    exp_old = jnp.exp(scores_old - peak[:, :, None])
    exp_new = jnp.exp(scores_new - peak)
    denom = jnp.sum(exp_old, axis=2) + exp_new
    probs_old = (exp_old / denom[:, :, None]).astype(jnp.bfloat16)
    probs_new = (exp_new / denom).astype(jnp.bfloat16)
    mixed = jnp.einsum(
        "thp,tpc->thc", probs_old, cache[:, :, :KVL], preferred_element_type=jnp.float32
    )
    mixed = mixed + probs_new.astype(jnp.float32)[:, :, None] * new_entry[:, None, :KVL].astype(
        jnp.float32
    )
    attn_out = mixed.astype(jnp.bfloat16)
    return (hidden, new_entry, attn_out)


def solution(mesh):
    placed = (
        P(("sec", "dev"), None),
        P(),
        P(("sec", "dev"), None),
        P(("sec", "dev"), None),
        P(None, ("sec", "dev")),
        P(None, ("sec", "dev")),
        P(("sec", "dev"), None),
        P(),
        P(),
        P(),
        P(("sec", "dev"), None, None),
        P(("sec", "dev")),
        P(("sec", "dev"), None, None),
    )
    return jax.shard_map(
        on_device,
        mesh=mesh,
        in_specs=placed,
        out_specs=(P(("sec", "dev"), None), P(("sec", "dev"), None), P(("sec", "dev"), None, None)),
        check_vma=False,
    )
```

```python
import functools

import jax
import jax.numpy as jnp
from jax import lax
from jax.experimental import pallas as pl
from jax.experimental.pallas import tpu as pltpu
from jax.sharding import PartitionSpec as P

KVL = 512
EXPERTS = 16
AXES = ("sec", "dev")
SIDE = 4
STRIDE = {"x": 16, "y": 4, "z": 1}
PLANE = (("x", "y"), ("y", "z"))
LINE = ("z", "x")
LANES = 128


norm_eps = 1e-06
SCORE_SCALE = 0.0721687836


def rms_scale(values, gain_vec):
    values = values.astype(jnp.float32)
    return (
        values * lax.rsqrt(jnp.mean(values * values, axis=-1, keepdims=True) + norm_eps) * gain_vec
    )


def rotate_half(rotary, positions):
    half_dim = rotary.shape[-1] // 2
    inv_freq = jnp.exp(
        -jnp.log(10000.0) * jnp.arange(half_dim).astype(jnp.float32) * 2.0 / rotary.shape[-1]
    )
    angles = positions.astype(jnp.float32)[:, None] * inv_freq[None, :]
    lower_half = rotary[:, :half_dim]
    upper_half = rotary[:, half_dim:]
    cosine = jnp.cos(angles)
    sine_val = jnp.sin(angles)
    return jnp.concatenate(
        [lower_half * cosine - upper_half * sine_val, upper_half * cosine + lower_half * sine_val],
        axis=-1,
    )


def shift(values, amount):
    pairs = []
    for sec in range(2):
        stride = STRIDE[LINE[sec]]
        for dev in range(SIDE**3):
            place = dev // stride % SIDE
            there = dev + ((place + amount) % SIDE - place) * stride
            pairs.append((sec * SIDE**3 + dev, sec * SIDE**3 + there))
    return lax.ppermute(values, AXES, pairs)


def plane_exchange(blocks):
    groups = []
    for sec in range(2):
        one, two = (STRIDE[axis] for axis in PLANE[sec])
        for line in range(SIDE):
            base = sec * SIDE**3 + line * STRIDE[LINE[sec]]
            groups.append([base + i * one + j * two for i in range(SIDE) for j in range(SIDE)])
    return lax.all_to_all(
        blocks, AXES, split_axis=0, concat_axis=0, axis_index_groups=groups, tiled=True
    )


def swap_cores(values):
    return lax.ppermute(values, AXES, [(i, (i + SIDE**3) % (2 * SIDE**3)) for i in range(2 * SIDE**3)])


def after(values, *earlier):
    return lax.optimization_barrier((values, *earlier))[0]


def act_body(info_ref, *refs):
    rows, weights, out_ref = refs[:-5], refs[-5:-1], refs[-1]
    depth, wide = weights[0].shape
    held = jnp.concatenate([part[:, depth:] for part in rows], axis=0).astype(jnp.float32)
    lane = lax.broadcasted_iota(jnp.int32, (1, LANES), 1)

    def product(which):
        left = jnp.concatenate([part[:, :depth] for part in rows], axis=0)
        return jnp.dot(left, weights[which][...], preferred_element_type=jnp.float32)

    for which in range(2):
        expert = info_ref[which]
        hit = (lane == expert) | (lane == expert + EXPERTS) | (lane == expert + 2 * EXPERTS)
        weight = jnp.sum(jnp.where(hit, held, 0.0), axis=1, keepdims=True)
        gate = product(which)
        up = product(2 + which)
        act = gate / (1.0 + jnp.exp(-gate)) * up * weight
        out_ref[:, which * wide : (which + 1) * wide] = act.astype(jnp.bfloat16)


def expert_acts(info, rows, weights):
    tokens = sum(part.shape[0] for part in rows)
    depth, wide = weights[0].shape
    vmem = pl.BlockSpec(memory_space=pltpu.VMEM)
    return pl.pallas_call(
        act_body,
        out_shape=jax.ShapeDtypeStruct((tokens, 2 * wide), jnp.bfloat16),
        in_specs=[pl.BlockSpec(memory_space=pltpu.SMEM)] + [vmem] * (len(rows) + 4),
        out_specs=vmem,
        compiler_params=pltpu.CompilerParams(vmem_limit_bytes=23 << 20),
        cost_estimate=pl.CostEstimate(
            flops=8 * tokens * depth * wide, bytes_accessed=1 << 20, transcendentals=0
        ),
        name="expert_acts",
    )(info, *rows, *weights)


def down_body(acts_ref, mine_ref, other_ref, *outs):
    wide = mine_ref.shape[0]
    group = outs[0].shape[0]
    step = 4 * LANES
    for low in range(0, mine_ref.shape[1], step):
        high = low + step
        part = jnp.dot(
            acts_ref[:, :wide], mine_ref[:, low:high], preferred_element_type=jnp.float32
        ) + jnp.dot(acts_ref[:, wide:], other_ref[:, low:high], preferred_element_type=jnp.float32)
        part = part.astype(jnp.bfloat16)
        for number, out in enumerate(outs):
            out[:, low:high] = part[number * group : (number + 1) * group]


def expert_outs(acts, mine, other, count):
    tokens, both = acts.shape
    width = mine.shape[1]
    vmem = pl.BlockSpec(memory_space=pltpu.VMEM)
    return pl.pallas_call(
        down_body,
        out_shape=[jax.ShapeDtypeStruct((tokens // count, width), jnp.bfloat16)] * count,
        in_specs=[vmem] * 3,
        out_specs=[vmem] * count,
        compiler_params=pltpu.CompilerParams(vmem_limit_bytes=16 << 20),
        cost_estimate=pl.CostEstimate(
            flops=2 * tokens * both * width, bytes_accessed=1 << 20, transcendentals=0
        ),
        name="expert_outs",
    )(acts, mine, other)


def plus(first, *others):
    total = first.astype(jnp.float32)
    for other in others:
        total = total + other.astype(jnp.float32)
    return total


def on_device(
    resid,
    ffn_gain,
    expert_ids,
    gate_weights,
    w_gate,
    w_up,
    w_down,
    attn_gain,
    w_kv,
    kv_gain,
    cache,
    lengths,
    queries,
):
    tok_count = resid.shape[0]
    model_width = resid.shape[1]
    sec = lax.axis_index("sec")
    chip_expert = lax.axis_index("dev") // (SIDE**3 // (EXPERTS // 2))
    gate_other = swap_cores(w_gate)
    normed = rms_scale(resid, ffn_gain).astype(jnp.bfloat16)
    dense_weights = jnp.sum(
        jnp.where(
            expert_ids[:, :, None] == jnp.arange(EXPERTS, dtype=jnp.int32)[None, None, :],
            gate_weights[:, :, None],
            0.0,
        ),
        axis=1,
    )
    high = dense_weights.astype(jnp.bfloat16)
    rest = dense_weights - high.astype(jnp.float32)
    middle = rest.astype(jnp.bfloat16)
    low = (rest - middle.astype(jnp.float32)).astype(jnp.bfloat16)
    weight_cols = jnp.concatenate(
        [high, middle, low, jnp.zeros((tok_count, LANES - 3 * EXPERTS), jnp.bfloat16)], axis=1
    )
    rows = jnp.concatenate([normed, weight_cols], axis=1)
    up_other = swap_cores(w_up)
    rows = plane_exchange(jnp.broadcast_to(rows[None], (SIDE * SIDE, *rows.shape)))
    rows, gate_other, up_other = lax.optimization_barrier((rows, gate_other, up_other))
    down_other = swap_cores(after(w_down, rows))
    low, high = jnp.split(rows, 2, axis=0)
    low_back, high_ahead = shift(low, 1), shift(high, -1)
    high_back, low_ahead = shift(high, 1), shift(low, -1)

    half = EXPERTS // 2
    info = jnp.stack([chip_expert + sec * half, chip_expert + (1 - sec) * half]).astype(jnp.int32)
    weights = (w_gate, gate_other, w_up, up_other)

    def flat(*parts):
        return [part.reshape(-1, part.shape[-1]) for part in parts]

    mine_acts = expert_acts(info, flat(rows), weights)
    low_back, high_ahead = lax.optimization_barrier((low_back, high_ahead, mine_acts))[:2]
    low_far, high_far = shift(low_back, 1), shift(high_ahead, -1)
    near_acts = expert_acts(info, flat(low_back, high_ahead), weights)
    acts = expert_acts(after(info, near_acts), flat(high_back, low_ahead), weights)
    high_back, low_ahead = expert_outs(acts, w_down, down_other, 2)
    high_back, low_ahead, low_far, high_far = lax.optimization_barrier(
        (high_back, low_ahead, low_far, high_far)
    )
    high_back, low_ahead = shift(high_back, -1), shift(low_ahead, 1)
    acts = expert_acts(info, flat(low_far, high_far), weights)
    low_far, high_far = expert_outs(acts, w_down, down_other, 2)
    low_far, high_far, high_back, low_ahead = lax.optimization_barrier(
        (low_far, high_far, high_back, low_ahead)
    )
    near_acts, mine_acts = lax.optimization_barrier((near_acts, mine_acts, low_far))[:2]
    low_far, high_far = shift(low_far, -1), shift(high_far, 1)
    low_back, high_ahead = expert_outs(near_acts, w_down, down_other, 2)
    low_mine, high_mine = expert_outs(mine_acts, w_down, down_other, 2)
    low_back = shift(plus(low_back, low_far).astype(jnp.bfloat16), -1)
    high_ahead = shift(plus(high_ahead, high_far).astype(jnp.bfloat16), 1)
    low = plus(low_mine, low_back, low_ahead).astype(jnp.bfloat16)
    high = plus(high_mine, high_back, high_ahead).astype(jnp.bfloat16)
    sums = jnp.concatenate([low, high], axis=0).reshape(SIDE * SIDE, tok_count, model_width)
    moe = jnp.sum(plane_exchange(sums).astype(jnp.float32), axis=0)
    hidden = (resid.astype(jnp.float32) + moe).astype(jnp.bfloat16)
    attn_in = rms_scale(hidden, attn_gain).astype(jnp.bfloat16)
    kv_raw = jnp.dot(attn_in, w_kv, preferred_element_type=jnp.float32)
    latent = rms_scale(kv_raw[:, :KVL], kv_gain)
    rotated = rotate_half(kv_raw[:, KVL:], lengths)
    new_entry = jnp.concatenate([latent, rotated], axis=-1).astype(jnp.bfloat16)
    scores_old = (
        jnp.einsum("thc,tpc->thp", queries, cache, preferred_element_type=jnp.float32) * SCORE_SCALE
    )
    scores_new = (
        jnp.einsum("thc,tc->th", queries, new_entry, preferred_element_type=jnp.float32)
        * SCORE_SCALE
    )
    live_mask = jnp.arange(cache.shape[1], dtype=jnp.int32)[None, None, :] < lengths[:, None, None]
    scores_old = jnp.where(live_mask, scores_old, -jnp.inf)
    peak = jnp.maximum(jnp.max(scores_old, axis=2), scores_new)
    exp_old = jnp.exp(scores_old - peak[:, :, None])
    exp_new = jnp.exp(scores_new - peak)
    denom = jnp.sum(exp_old, axis=2) + exp_new
    probs_old = (exp_old / denom[:, :, None]).astype(jnp.bfloat16)
    probs_new = (exp_new / denom).astype(jnp.bfloat16)
    mixed = jnp.einsum(
        "thp,tpc->thc", probs_old, cache[:, :, :KVL], preferred_element_type=jnp.float32
    )
    mixed = mixed + probs_new.astype(jnp.float32)[:, :, None] * new_entry[:, None, :KVL].astype(
        jnp.float32
    )
    attn_out = mixed.astype(jnp.bfloat16)
    return (hidden, new_entry, attn_out)


def solution(mesh):
    placed = (
        P(("sec", "dev"), None),
        P(),
        P(("sec", "dev"), None),
        P(("sec", "dev"), None),
        P(None, ("sec", "dev")),
        P(None, ("sec", "dev")),
        P(("sec", "dev"), None),
        P(),
        P(),
        P(),
        P(("sec", "dev"), None, None),
        P(("sec", "dev")),
        P(("sec", "dev"), None, None),
    )
    return jax.shard_map(
        on_device,
        mesh=mesh,
        in_specs=placed,
        out_specs=(P(("sec", "dev"), None), P(("sec", "dev"), None), P(("sec", "dev"), None, None)),
        check_vma=False,
    )
```

```python
import functools

import jax
import jax.numpy as jnp
from jax import lax
from jax.experimental import pallas as pl
from jax.experimental.pallas import tpu as pltpu
from jax.sharding import PartitionSpec as P

KVL = 512
EXPERTS = 16
AXES = ("sec", "dev")
SIDE = 4
STRIDE = {"x": 16, "y": 4, "z": 1}
ORDER = (("x", "y", "z"), ("y", "z", "x"))
LANES = 128


norm_eps = 1e-06
SCORE_SCALE = 0.0721687836


def rms_scale(values, gain_vec):
    values = values.astype(jnp.float32)
    return (
        values * lax.rsqrt(jnp.mean(values * values, axis=-1, keepdims=True) + norm_eps) * gain_vec
    )


def rotate_half(rotary, positions):
    half_dim = rotary.shape[-1] // 2
    inv_freq = jnp.exp(
        -jnp.log(10000.0) * jnp.arange(half_dim).astype(jnp.float32) * 2.0 / rotary.shape[-1]
    )
    angles = positions.astype(jnp.float32)[:, None] * inv_freq[None, :]
    lower_half = rotary[:, :half_dim]
    upper_half = rotary[:, half_dim:]
    cosine = jnp.cos(angles)
    sine_val = jnp.sin(angles)
    return jnp.concatenate(
        [lower_half * cosine - upper_half * sine_val, upper_half * cosine + lower_half * sine_val],
        axis=-1,
    )


def shift(values, phase, amount):
    pairs = []
    for sec in range(2):
        stride = STRIDE[ORDER[sec][phase]]
        for dev in range(SIDE**3):
            place = dev // stride % SIDE
            there = dev + ((place + amount) % SIDE - place) * stride
            pairs.append((sec * SIDE**3 + dev, sec * SIDE**3 + there))
    return lax.ppermute(values, AXES, pairs)


def swap_cores(values):
    return lax.ppermute(values, AXES, [(i, (i + SIDE**3) % (2 * SIDE**3)) for i in range(2 * SIDE**3)])


def after(values, *earlier):
    return lax.optimization_barrier((values, *earlier))[0]


def join_body(count, *refs):
    ins, outs, sems = refs[:SIDE], refs[SIDE : SIDE + count], refs[-1]
    each = SIDE // count
    copies = []
    for back in range(SIDE):
        rows = ins[back].shape[0]
        copies.append(
            pltpu.make_async_copy(
                ins[back],
                outs[back // each].at[pl.ds(back % each * rows, rows)],
                sems.at[back],
            )
        )
    for copy in copies:
        copy.start()
    for copy in copies:
        copy.wait()


def join(blocks, count):
    rows, *rest = blocks[0].shape
    hbm = pl.BlockSpec(memory_space=pl.ANY)
    return pl.pallas_call(
        functools.partial(join_body, count),
        out_shape=[jax.ShapeDtypeStruct((SIDE // count * rows, *rest), blocks[0].dtype)] * count,
        in_specs=[hbm] * SIDE,
        out_specs=[hbm] * count,
        scratch_shapes=[pltpu.SemaphoreType.DMA((SIDE,))],
        compiler_params=pltpu.CompilerParams(vmem_limit_bytes=1 << 20),
        name="join",
    )(*blocks)


def act_body(info_ref, *refs):
    rows, weights, out_ref = refs[:-5], refs[-5:-1], refs[-1]
    depth, wide = weights[0].shape
    held = jnp.concatenate([part[:, depth:] for part in rows], axis=0).astype(jnp.float32)
    lane = lax.broadcasted_iota(jnp.int32, (1, LANES), 1)

    def product(which):
        left = jnp.concatenate([part[:, :depth] for part in rows], axis=0)
        return jnp.dot(left, weights[which][...], preferred_element_type=jnp.float32)

    for which in range(2):
        expert = info_ref[which]
        hit = (lane == expert) | (lane == expert + EXPERTS) | (lane == expert + 2 * EXPERTS)
        weight = jnp.sum(jnp.where(hit, held, 0.0), axis=1, keepdims=True)
        gate = product(which)
        up = product(2 + which)
        act = gate / (1.0 + jnp.exp(-gate)) * up * weight
        out_ref[:, which * wide : (which + 1) * wide] = act.astype(jnp.bfloat16)


def expert_acts(info, rows, weights):
    tokens = sum(part.shape[0] for part in rows)
    depth, wide = weights[0].shape
    vmem = pl.BlockSpec(memory_space=pltpu.VMEM)
    return pl.pallas_call(
        act_body,
        out_shape=jax.ShapeDtypeStruct((tokens, 2 * wide), jnp.bfloat16),
        in_specs=[pl.BlockSpec(memory_space=pltpu.SMEM)] + [vmem] * (len(rows) + 4),
        out_specs=vmem,
        compiler_params=pltpu.CompilerParams(vmem_limit_bytes=18 << 20),
        cost_estimate=pl.CostEstimate(
            flops=8 * tokens * depth * wide, bytes_accessed=1 << 20, transcendentals=0
        ),
        name="expert_acts",
    )(info, *rows, *weights)


def down_body(acts_ref, mine_ref, other_ref, *outs):
    wide = mine_ref.shape[0]
    group = outs[0].shape[0]
    step = 4 * LANES
    for low in range(0, mine_ref.shape[1], step):
        high = low + step
        part = jnp.dot(
            acts_ref[:, :wide], mine_ref[:, low:high], preferred_element_type=jnp.float32
        ) + jnp.dot(acts_ref[:, wide:], other_ref[:, low:high], preferred_element_type=jnp.float32)
        part = part.astype(jnp.bfloat16)
        for number, out in enumerate(outs):
            out[:, low:high] = part[number * group : (number + 1) * group]


def expert_outs(acts, mine, other, count):
    tokens, both = acts.shape
    width = mine.shape[1]
    vmem = pl.BlockSpec(memory_space=pltpu.VMEM)
    return pl.pallas_call(
        down_body,
        out_shape=[jax.ShapeDtypeStruct((tokens // count, width), jnp.bfloat16)] * count,
        in_specs=[vmem] * 3,
        out_specs=[vmem] * count,
        compiler_params=pltpu.CompilerParams(vmem_limit_bytes=18 << 20),
        cost_estimate=pl.CostEstimate(
            flops=2 * tokens * both * width, bytes_accessed=1 << 20, transcendentals=0
        ),
        name="expert_outs",
    )(acts, mine, other)


def plus(first, *others):
    total = first.astype(jnp.float32)
    for other in others:
        total = total + other.astype(jnp.float32)
    return total


def on_device(
    resid,
    ffn_gain,
    expert_ids,
    gate_weights,
    w_gate,
    w_up,
    w_down,
    attn_gain,
    w_kv,
    kv_gain,
    cache,
    lengths,
    queries,
):
    tok_count = resid.shape[0]
    model_width = resid.shape[1]
    sec = lax.axis_index("sec")
    chip_expert = lax.axis_index("dev") // (SIDE**3 // (EXPERTS // 2))
    gate_other = swap_cores(w_gate)
    normed = rms_scale(resid, ffn_gain).astype(jnp.bfloat16)
    dense_weights = jnp.sum(
        jnp.where(
            expert_ids[:, :, None] == jnp.arange(EXPERTS, dtype=jnp.int32)[None, None, :],
            gate_weights[:, :, None],
            0.0,
        ),
        axis=1,
    )
    high = dense_weights.astype(jnp.bfloat16)
    rest = dense_weights - high.astype(jnp.float32)
    middle = rest.astype(jnp.bfloat16)
    low = (rest - middle.astype(jnp.float32)).astype(jnp.bfloat16)
    weight_cols = jnp.concatenate(
        [high, middle, low, jnp.zeros((tok_count, LANES - 3 * EXPERTS), jnp.bfloat16)], axis=1
    )
    rows = jnp.concatenate([normed, weight_cols], axis=1)
    up_other = swap_cores(w_up)
    rows = rows[None]
    (rows,) = join([rows] + [shift(rows, 0, back) for back in range(1, SIDE)], 1)
    got = [rows] + [shift(rows, 1, back) for back in range(1, SIDE)]
    low, high = join(lax.optimization_barrier((got, gate_other, up_other))[0], 2)
    down_other = swap_cores(after(w_down, low))
    low_back, high_ahead = shift(low, 2, 1), shift(high, 2, -1)
    high_back, low_ahead = shift(high, 2, 1), shift(low, 2, -1)

    half = EXPERTS // 2
    info = jnp.stack([chip_expert + sec * half, chip_expert + (1 - sec) * half]).astype(jnp.int32)
    weights = (w_gate, gate_other, w_up, up_other)

    def acts_of(number, *parts):
        return expert_acts(number, [part.reshape(-1, part.shape[-1]) for part in parts], weights)

    def outs_of(acts):
        return expert_outs(acts, w_down, down_other, 2)

    mine_acts = acts_of(info, low, high)
    low_back, high_ahead = lax.optimization_barrier((low_back, high_ahead, mine_acts))[:2]
    low_far, high_far = shift(low_back, 2, 1), shift(high_ahead, 2, -1)
    near_rows = (low_back, high_ahead)
    high_back, low_ahead = outs_of(acts_of(info, high_back, low_ahead))
    high_back, low_ahead, low_far, high_far = lax.optimization_barrier(
        (high_back, low_ahead, low_far, high_far)
    )
    high_back, low_ahead = shift(high_back, 2, -1), shift(low_ahead, 2, 1)
    low_far, high_far = outs_of(acts_of(info, low_far, high_far))
    near_info = after(info, low_far)
    low_far, high_far, high_back, low_ahead = lax.optimization_barrier(
        (low_far, high_far, high_back, low_ahead)
    )
    low_far, high_far = shift(low_far, 2, -1), shift(high_far, 2, 1)
    low_back, high_ahead = outs_of(acts_of(near_info, *near_rows))
    low_mine, high_mine = outs_of(after(mine_acts, low_back))
    low_back, high_ahead = lax.optimization_barrier(
        (
            plus(low_back, low_far).astype(jnp.bfloat16),
            plus(high_ahead, high_far).astype(jnp.bfloat16),
        )
    )
    low_back, high_ahead = shift(low_back, 2, -1), shift(high_ahead, 2, 1)
    low = plus(low_mine, low_back, low_ahead).astype(jnp.bfloat16)
    high = plus(high_mine, high_back, high_ahead).astype(jnp.bfloat16)
    low, high = lax.optimization_barrier((low, high))
    parts = [*jnp.split(low, 2, axis=0), *jnp.split(high, 2, axis=0)]
    for phase in (1, 0):
        moe = plus(parts[0], *(shift(parts[back], phase, -back) for back in range(1, SIDE)))
        if phase > 0:
            parts = jnp.split(moe.astype(jnp.bfloat16), SIDE, axis=0)
    hidden = (resid.astype(jnp.float32) + moe).astype(jnp.bfloat16)
    attn_in = rms_scale(hidden, attn_gain).astype(jnp.bfloat16)
    kv_raw = jnp.dot(attn_in, w_kv, preferred_element_type=jnp.float32)
    latent = rms_scale(kv_raw[:, :KVL], kv_gain)
    rotated = rotate_half(kv_raw[:, KVL:], lengths)
    new_entry = jnp.concatenate([latent, rotated], axis=-1).astype(jnp.bfloat16)
    scores_old = (
        jnp.einsum("thc,tpc->thp", queries, cache, preferred_element_type=jnp.float32) * SCORE_SCALE
    )
    scores_new = (
        jnp.einsum("thc,tc->th", queries, new_entry, preferred_element_type=jnp.float32)
        * SCORE_SCALE
    )
    live_mask = jnp.arange(cache.shape[1], dtype=jnp.int32)[None, None, :] < lengths[:, None, None]
    scores_old = jnp.where(live_mask, scores_old, -jnp.inf)
    peak = jnp.maximum(jnp.max(scores_old, axis=2), scores_new)
    exp_old = jnp.exp(scores_old - peak[:, :, None])
    exp_new = jnp.exp(scores_new - peak)
    denom = jnp.sum(exp_old, axis=2) + exp_new
    probs_old = (exp_old / denom[:, :, None]).astype(jnp.bfloat16)
    probs_new = (exp_new / denom).astype(jnp.bfloat16)
    mixed = jnp.einsum(
        "thp,tpc->thc", probs_old, cache[:, :, :KVL], preferred_element_type=jnp.float32
    )
    mixed = mixed + probs_new.astype(jnp.float32)[:, :, None] * new_entry[:, None, :KVL].astype(
        jnp.float32
    )
    attn_out = mixed.astype(jnp.bfloat16)
    return (hidden, new_entry, attn_out)


def solution(mesh):
    placed = (
        P(("sec", "dev"), None),
        P(),
        P(("sec", "dev"), None),
        P(("sec", "dev"), None),
        P(None, ("sec", "dev")),
        P(None, ("sec", "dev")),
        P(("sec", "dev"), None),
        P(),
        P(),
        P(),
        P(("sec", "dev"), None, None),
        P(("sec", "dev")),
        P(("sec", "dev"), None, None),
    )
    return jax.shard_map(
        on_device,
        mesh=mesh,
        in_specs=placed,
        out_specs=(P(("sec", "dev"), None), P(("sec", "dev"), None), P(("sec", "dev"), None, None)),
        check_vma=False,
    )
```

```python
import functools

import jax
import jax.numpy as jnp
from jax import lax
from jax.experimental import pallas as pl
from jax.experimental.pallas import tpu as pltpu
from jax.sharding import PartitionSpec as P

KVL = 512
EXPERTS = 16
AXES = ("sec", "dev")
SIDE = 4
STRIDE = {"x": 16, "y": 4, "z": 1}
ORDER = (("x", "y", "z"), ("y", "z", "x"))
LANES = 128


norm_eps = 1e-06
SCORE_SCALE = 0.0721687836


def rms_scale(values, gain_vec):
    values = values.astype(jnp.float32)
    return (
        values * lax.rsqrt(jnp.mean(values * values, axis=-1, keepdims=True) + norm_eps) * gain_vec
    )


def rotate_half(rotary, positions):
    half_dim = rotary.shape[-1] // 2
    inv_freq = jnp.exp(
        -jnp.log(10000.0) * jnp.arange(half_dim).astype(jnp.float32) * 2.0 / rotary.shape[-1]
    )
    angles = positions.astype(jnp.float32)[:, None] * inv_freq[None, :]
    lower_half = rotary[:, :half_dim]
    upper_half = rotary[:, half_dim:]
    cosine = jnp.cos(angles)
    sine_val = jnp.sin(angles)
    return jnp.concatenate(
        [lower_half * cosine - upper_half * sine_val, upper_half * cosine + lower_half * sine_val],
        axis=-1,
    )


def shift(values, phase, amount):
    pairs = []
    for sec in range(2):
        stride = STRIDE[ORDER[sec][phase]]
        for dev in range(SIDE**3):
            place = dev // stride % SIDE
            there = dev + ((place + amount) % SIDE - place) * stride
            pairs.append((sec * SIDE**3 + dev, sec * SIDE**3 + there))
    return lax.ppermute(values, AXES, pairs)


def swap_cores(values):
    return lax.ppermute(values, AXES, [(i, (i + SIDE**3) % (2 * SIDE**3)) for i in range(2 * SIDE**3)])


def after(values, *earlier):
    return lax.optimization_barrier((values, *earlier))[0]


def join_body(count, *refs):
    ins, outs, sems = refs[:SIDE], refs[SIDE : SIDE + count], refs[-1]
    each = SIDE // count
    copies = []
    for back in range(SIDE):
        rows = ins[back].shape[0]
        copies.append(
            pltpu.make_async_copy(
                ins[back],
                outs[back // each].at[pl.ds(back % each * rows, rows)],
                sems.at[back],
            )
        )
    for copy in copies:
        copy.start()
    for copy in copies:
        copy.wait()


def join(blocks, count):
    rows, *rest = blocks[0].shape
    hbm = pl.BlockSpec(memory_space=pl.ANY)
    return pl.pallas_call(
        functools.partial(join_body, count),
        out_shape=[jax.ShapeDtypeStruct((SIDE // count * rows, *rest), blocks[0].dtype)] * count,
        in_specs=[hbm] * SIDE,
        out_specs=[hbm] * count,
        scratch_shapes=[pltpu.SemaphoreType.DMA((SIDE,))],
        compiler_params=pltpu.CompilerParams(vmem_limit_bytes=1 << 20),
        name="join",
    )(*blocks)


def act_body(info_ref, *refs):
    rows, weights, out_ref = refs[:-5], refs[-5:-1], refs[-1]
    depth, wide = weights[0].shape
    held = jnp.concatenate([part[:, depth:] for part in rows], axis=0).astype(jnp.float32)
    lane = lax.broadcasted_iota(jnp.int32, (1, LANES), 1)

    def product(which):
        left = jnp.concatenate([part[:, :depth] for part in rows], axis=0)
        return jnp.dot(left, weights[which][...], preferred_element_type=jnp.float32)

    for which in range(2):
        expert = info_ref[which]
        hit = (lane == expert) | (lane == expert + EXPERTS) | (lane == expert + 2 * EXPERTS)
        weight = jnp.sum(jnp.where(hit, held, 0.0), axis=1, keepdims=True)
        gate = product(which)
        up = product(2 + which)
        act = gate / (1.0 + jnp.exp(-gate)) * up * weight
        out_ref[:, which * wide : (which + 1) * wide] = act.astype(jnp.bfloat16)


def expert_acts(info, rows, weights):
    tokens = sum(part.shape[0] for part in rows)
    depth, wide = weights[0].shape
    vmem = pl.BlockSpec(memory_space=pltpu.VMEM)
    return pl.pallas_call(
        act_body,
        out_shape=jax.ShapeDtypeStruct((tokens, 2 * wide), jnp.bfloat16),
        in_specs=[pl.BlockSpec(memory_space=pltpu.SMEM)] + [vmem] * (len(rows) + 4),
        out_specs=vmem,
        compiler_params=pltpu.CompilerParams(vmem_limit_bytes=18 << 20),
        cost_estimate=pl.CostEstimate(
            flops=8 * tokens * depth * wide, bytes_accessed=1 << 20, transcendentals=0
        ),
        name="expert_acts",
    )(info, *rows, *weights)


def down_body(acts_ref, mine_ref, other_ref, *outs):
    wide = mine_ref.shape[0]
    group = outs[0].shape[0]
    step = 4 * LANES
    for low in range(0, mine_ref.shape[1], step):
        high = low + step
        part = jnp.dot(
            acts_ref[:, :wide], mine_ref[:, low:high], preferred_element_type=jnp.float32
        ) + jnp.dot(acts_ref[:, wide:], other_ref[:, low:high], preferred_element_type=jnp.float32)
        part = part.astype(jnp.bfloat16)
        for number, out in enumerate(outs):
            out[:, low:high] = part[number * group : (number + 1) * group]


def expert_outs(acts, mine, other, count):
    tokens, both = acts.shape
    width = mine.shape[1]
    vmem = pl.BlockSpec(memory_space=pltpu.VMEM)
    return pl.pallas_call(
        down_body,
        out_shape=[jax.ShapeDtypeStruct((tokens // count, width), jnp.bfloat16)] * count,
        in_specs=[vmem] * 3,
        out_specs=[vmem] * count,
        compiler_params=pltpu.CompilerParams(vmem_limit_bytes=18 << 20),
        cost_estimate=pl.CostEstimate(
            flops=2 * tokens * both * width, bytes_accessed=1 << 20, transcendentals=0
        ),
        name="expert_outs",
    )(acts, mine, other)


def plus(first, *others):
    total = first.astype(jnp.float32)
    for other in others:
        total = total + other.astype(jnp.float32)
    return total


def on_device(
    resid,
    ffn_gain,
    expert_ids,
    gate_weights,
    w_gate,
    w_up,
    w_down,
    attn_gain,
    w_kv,
    kv_gain,
    cache,
    lengths,
    queries,
):
    tok_count = resid.shape[0]
    model_width = resid.shape[1]
    sec = lax.axis_index("sec")
    chip_expert = lax.axis_index("dev") // (SIDE**3 // (EXPERTS // 2))
    gate_other = swap_cores(w_gate)
    normed = rms_scale(resid, ffn_gain).astype(jnp.bfloat16)
    dense_weights = jnp.sum(
        jnp.where(
            expert_ids[:, :, None] == jnp.arange(EXPERTS, dtype=jnp.int32)[None, None, :],
            gate_weights[:, :, None],
            0.0,
        ),
        axis=1,
    )
    high = dense_weights.astype(jnp.bfloat16)
    rest = dense_weights - high.astype(jnp.float32)
    middle = rest.astype(jnp.bfloat16)
    low = (rest - middle.astype(jnp.float32)).astype(jnp.bfloat16)
    weight_cols = jnp.concatenate(
        [high, middle, low, jnp.zeros((tok_count, LANES - 3 * EXPERTS), jnp.bfloat16)], axis=1
    )
    rows = jnp.concatenate([normed, weight_cols], axis=1)
    up_other = swap_cores(w_up)
    rows = rows[None]
    (rows,) = join([rows] + [shift(rows, 0, back) for back in range(1, SIDE)], 1)
    got = [rows] + [shift(rows, 1, back) for back in range(1, SIDE)]
    low, high = join(lax.optimization_barrier((got, gate_other, up_other))[0], 2)
    down_other = swap_cores(after(w_down, low))
    low_back, high_ahead = shift(low, 2, 1), shift(high, 2, -1)
    high_back, low_ahead = shift(high, 2, 1), shift(low, 2, -1)

    half = EXPERTS // 2
    info = jnp.stack([chip_expert + sec * half, chip_expert + (1 - sec) * half]).astype(jnp.int32)
    weights = (w_gate, gate_other, w_up, up_other)

    def acts_of(number, *parts):
        return expert_acts(number, [part.reshape(-1, part.shape[-1]) for part in parts], weights)

    def outs_of(acts):
        return expert_outs(acts, w_down, down_other, 2)

    mine_acts = acts_of(info, low, high)
    low_back, high_ahead = lax.optimization_barrier((low_back, high_ahead, mine_acts))[:2]
    low_far, high_far = shift(low_back, 2, 1), shift(high_ahead, 2, -1)
    near_acts = acts_of(info, high_back, low_ahead, low_back, high_ahead)
    middle = near_acts.shape[0] // 2
    high_back, low_ahead = outs_of(near_acts[:middle])
    high_back = shift(after(high_back, high_far), 2, -1)
    low_ahead = shift(after(low_ahead, low_far), 2, 1)
    low_far, high_far = outs_of(acts_of(info, low_far, high_far))
    near_acts, mine_acts = lax.optimization_barrier((near_acts, mine_acts, low_far))[:2]
    low_far = shift(after(low_far, high_back), 2, -1)
    high_far = shift(after(high_far, low_ahead), 2, 1)
    low_back, high_ahead = outs_of(near_acts[middle:])
    low_mine, high_mine = outs_of(mine_acts)
    low_back = after(plus(low_back, low_far).astype(jnp.bfloat16), low_mine)
    high_ahead = after(plus(high_ahead, high_far).astype(jnp.bfloat16), low_mine)
    low_back, high_ahead = shift(low_back, 2, -1), shift(high_ahead, 2, 1)
    low = plus(low_mine, low_back, low_ahead).astype(jnp.bfloat16)
    high = plus(high_mine, high_back, high_ahead).astype(jnp.bfloat16)
    low, high = lax.optimization_barrier((low, high))
    parts = [*jnp.split(low, 2, axis=0), *jnp.split(high, 2, axis=0)]
    for phase in (1, 0):
        moe = plus(parts[0], *(shift(parts[back], phase, -back) for back in range(1, SIDE)))
        if phase > 0:
            parts = jnp.split(moe.astype(jnp.bfloat16), SIDE, axis=0)
    hidden = (resid.astype(jnp.float32) + moe).astype(jnp.bfloat16)
    attn_in = rms_scale(hidden, attn_gain).astype(jnp.bfloat16)
    kv_raw = jnp.dot(attn_in, w_kv, preferred_element_type=jnp.float32)
    latent = rms_scale(kv_raw[:, :KVL], kv_gain)
    rotated = rotate_half(kv_raw[:, KVL:], lengths)
    new_entry = jnp.concatenate([latent, rotated], axis=-1).astype(jnp.bfloat16)
    scores_old = (
        jnp.einsum("thc,tpc->thp", queries, cache, preferred_element_type=jnp.float32) * SCORE_SCALE
    )
    scores_new = (
        jnp.einsum("thc,tc->th", queries, new_entry, preferred_element_type=jnp.float32)
        * SCORE_SCALE
    )
    live_mask = jnp.arange(cache.shape[1], dtype=jnp.int32)[None, None, :] < lengths[:, None, None]
    scores_old = jnp.where(live_mask, scores_old, -jnp.inf)
    peak = jnp.maximum(jnp.max(scores_old, axis=2), scores_new)
    exp_old = jnp.exp(scores_old - peak[:, :, None])
    exp_new = jnp.exp(scores_new - peak)
    denom = jnp.sum(exp_old, axis=2) + exp_new
    probs_old = (exp_old / denom[:, :, None]).astype(jnp.bfloat16)
    probs_new = (exp_new / denom).astype(jnp.bfloat16)
    mixed = jnp.einsum(
        "thp,tpc->thc", probs_old, cache[:, :, :KVL], preferred_element_type=jnp.float32
    )
    mixed = mixed + probs_new.astype(jnp.float32)[:, :, None] * new_entry[:, None, :KVL].astype(
        jnp.float32
    )
    attn_out = mixed.astype(jnp.bfloat16)
    return (hidden, new_entry, attn_out)


def solution(mesh):
    placed = (
        P(("sec", "dev"), None),
        P(),
        P(("sec", "dev"), None),
        P(("sec", "dev"), None),
        P(None, ("sec", "dev")),
        P(None, ("sec", "dev")),
        P(("sec", "dev"), None),
        P(),
        P(),
        P(),
        P(("sec", "dev"), None, None),
        P(("sec", "dev")),
        P(("sec", "dev"), None, None),
    )
    return jax.shard_map(
        on_device,
        mesh=mesh,
        in_specs=placed,
        out_specs=(P(("sec", "dev"), None), P(("sec", "dev"), None), P(("sec", "dev"), None, None)),
        check_vma=False,
    )
```

```python
import functools

import jax
import jax.numpy as jnp
from jax import lax
from jax.experimental import pallas as pl
from jax.experimental.pallas import tpu as pltpu
from jax.sharding import PartitionSpec as P

KVL = 512
EXPERTS = 16
AXES = ("sec", "dev")
SIDE = 4
STRIDE = {"x": 16, "y": 4, "z": 1}
ORDER = (("x", "y", "z"), ("y", "z", "x"))
LANES = 128


norm_eps = 1e-06
SCORE_SCALE = 0.0721687836


def rms_scale(values, gain_vec):
    values = values.astype(jnp.float32)
    return (
        values * lax.rsqrt(jnp.mean(values * values, axis=-1, keepdims=True) + norm_eps) * gain_vec
    )


def rotate_half(rotary, positions):
    half_dim = rotary.shape[-1] // 2
    inv_freq = jnp.exp(
        -jnp.log(10000.0) * jnp.arange(half_dim).astype(jnp.float32) * 2.0 / rotary.shape[-1]
    )
    angles = positions.astype(jnp.float32)[:, None] * inv_freq[None, :]
    lower_half = rotary[:, :half_dim]
    upper_half = rotary[:, half_dim:]
    cosine = jnp.cos(angles)
    sine_val = jnp.sin(angles)
    return jnp.concatenate(
        [lower_half * cosine - upper_half * sine_val, upper_half * cosine + lower_half * sine_val],
        axis=-1,
    )


def shift(values, phase, amount):
    pairs = []
    for sec in range(2):
        stride = STRIDE[ORDER[sec][phase]]
        for dev in range(SIDE**3):
            place = dev // stride % SIDE
            there = dev + ((place + amount) % SIDE - place) * stride
            pairs.append((sec * SIDE**3 + dev, sec * SIDE**3 + there))
    return lax.ppermute(values, AXES, pairs)


def swap_cores(values):
    return lax.ppermute(values, AXES, [(i, (i + SIDE**3) % (2 * SIDE**3)) for i in range(2 * SIDE**3)])


def after(values, *earlier):
    return lax.optimization_barrier((values, *earlier))[0]


def join_body(count, *refs):
    ins, outs, sems = refs[:SIDE], refs[SIDE : SIDE + count], refs[-1]
    each = SIDE // count
    copies = []
    for back in range(SIDE):
        rows = ins[back].shape[0]
        copies.append(
            pltpu.make_async_copy(
                ins[back],
                outs[back // each].at[pl.ds(back % each * rows, rows)],
                sems.at[back],
            )
        )
    for copy in copies:
        copy.start()
    for copy in copies:
        copy.wait()


def join(blocks, count):
    rows, *rest = blocks[0].shape
    hbm = pl.BlockSpec(memory_space=pl.ANY)
    return pl.pallas_call(
        functools.partial(join_body, count),
        out_shape=[jax.ShapeDtypeStruct((SIDE // count * rows, *rest), blocks[0].dtype)] * count,
        in_specs=[hbm] * SIDE,
        out_specs=[hbm] * count,
        scratch_shapes=[pltpu.SemaphoreType.DMA((SIDE,))],
        compiler_params=pltpu.CompilerParams(vmem_limit_bytes=1 << 20),
        name="join",
    )(*blocks)


def act_body(info_ref, *refs):
    rows, weights, out_ref = refs[:-5], refs[-5:-1], refs[-1]
    depth, wide = weights[0].shape
    held = jnp.concatenate([part[:, depth:] for part in rows], axis=0).astype(jnp.float32)
    lane = lax.broadcasted_iota(jnp.int32, (1, LANES), 1)

    def product(which):
        left = jnp.concatenate([part[:, :depth] for part in rows], axis=0)
        return jnp.dot(left, weights[which][...], preferred_element_type=jnp.float32)

    for which in range(2):
        expert = info_ref[which]
        hit = (lane == expert) | (lane == expert + EXPERTS) | (lane == expert + 2 * EXPERTS)
        weight = jnp.sum(jnp.where(hit, held, 0.0), axis=1, keepdims=True)
        gate = product(which)
        up = product(2 + which)
        act = gate / (1.0 + jnp.exp(-gate)) * up * weight
        out_ref[:, which * wide : (which + 1) * wide] = act.astype(jnp.bfloat16)


def expert_acts(info, rows, weights):
    tokens = sum(part.shape[0] for part in rows)
    depth, wide = weights[0].shape
    vmem = pl.BlockSpec(memory_space=pltpu.VMEM)
    return pl.pallas_call(
        act_body,
        out_shape=jax.ShapeDtypeStruct((tokens, 2 * wide), jnp.bfloat16),
        in_specs=[pl.BlockSpec(memory_space=pltpu.SMEM)] + [vmem] * (len(rows) + 4),
        out_specs=vmem,
        compiler_params=pltpu.CompilerParams(vmem_limit_bytes=18 << 20),
        cost_estimate=pl.CostEstimate(
            flops=8 * tokens * depth * wide, bytes_accessed=1 << 20, transcendentals=0
        ),
        name="expert_acts",
    )(info, *rows, *weights)


def down_body(acts_ref, mine_ref, other_ref, *outs):
    wide = mine_ref.shape[0]
    group = outs[0].shape[0]
    step = 4 * LANES
    for low in range(0, mine_ref.shape[1], step):
        high = low + step
        part = jnp.dot(
            acts_ref[:, :wide], mine_ref[:, low:high], preferred_element_type=jnp.float32
        ) + jnp.dot(acts_ref[:, wide:], other_ref[:, low:high], preferred_element_type=jnp.float32)
        part = part.astype(jnp.bfloat16)
        for number, out in enumerate(outs):
            out[:, low:high] = part[number * group : (number + 1) * group]


def expert_outs(acts, mine, other, count):
    tokens, both = acts.shape
    width = mine.shape[1]
    vmem = pl.BlockSpec(memory_space=pltpu.VMEM)
    return pl.pallas_call(
        down_body,
        out_shape=[jax.ShapeDtypeStruct((tokens // count, width), jnp.bfloat16)] * count,
        in_specs=[vmem] * 3,
        out_specs=[vmem] * count,
        compiler_params=pltpu.CompilerParams(vmem_limit_bytes=18 << 20),
        cost_estimate=pl.CostEstimate(
            flops=2 * tokens * both * width, bytes_accessed=1 << 20, transcendentals=0
        ),
        name="expert_outs",
    )(acts, mine, other)


def plus(first, *others):
    total = first.astype(jnp.float32)
    for other in others:
        total = total + other.astype(jnp.float32)
    return total


def on_device(
    resid,
    ffn_gain,
    expert_ids,
    gate_weights,
    w_gate,
    w_up,
    w_down,
    attn_gain,
    w_kv,
    kv_gain,
    cache,
    lengths,
    queries,
):
    tok_count = resid.shape[0]
    model_width = resid.shape[1]
    sec = lax.axis_index("sec")
    chip_expert = lax.axis_index("dev") // (SIDE**3 // (EXPERTS // 2))
    gate_other = swap_cores(w_gate)
    normed = rms_scale(resid, ffn_gain).astype(jnp.bfloat16)
    dense_weights = jnp.sum(
        jnp.where(
            expert_ids[:, :, None] == jnp.arange(EXPERTS, dtype=jnp.int32)[None, None, :],
            gate_weights[:, :, None],
            0.0,
        ),
        axis=1,
    )
    high = dense_weights.astype(jnp.bfloat16)
    rest = dense_weights - high.astype(jnp.float32)
    middle = rest.astype(jnp.bfloat16)
    low = (rest - middle.astype(jnp.float32)).astype(jnp.bfloat16)
    weight_cols = jnp.concatenate(
        [high, middle, low, jnp.zeros((tok_count, LANES - 3 * EXPERTS), jnp.bfloat16)], axis=1
    )
    rows = jnp.concatenate([normed, weight_cols], axis=1)
    up_other = swap_cores(w_up)
    rows = rows[None]
    (rows,) = join([rows] + [shift(rows, 0, back) for back in range(1, SIDE)], 1)
    got = [rows] + [shift(rows, 1, back) for back in range(1, SIDE)]
    low, high = join(lax.optimization_barrier((got, gate_other, up_other))[0], 2)
    down_other = swap_cores(after(w_down, low))
    low_back, high_ahead = shift(low, 2, 1), shift(high, 2, -1)
    high_back, low_ahead = shift(high, 2, 1), shift(low, 2, -1)

    half = EXPERTS // 2
    info = jnp.stack([chip_expert + sec * half, chip_expert + (1 - sec) * half]).astype(jnp.int32)
    weights = (w_gate, gate_other, w_up, up_other)

    def acts_of(number, *parts):
        return expert_acts(number, [part.reshape(-1, part.shape[-1]) for part in parts], weights)

    def outs_of(acts):
        return expert_outs(acts, w_down, down_other, 2)

    mine_acts = acts_of(info, low, high)
    low_back, high_ahead = lax.optimization_barrier((low_back, high_ahead, mine_acts))[:2]
    low_far, high_far = shift(low_back, 2, 1), shift(high_ahead, 2, -1)
    near_acts = acts_of(info, low_back, high_ahead)
    near_acts, high_back, low_ahead = lax.optimization_barrier((near_acts, high_back, low_ahead))
    low_back, high_ahead = outs_of(near_acts)
    low_back = shift(after(low_back, high_far), 2, -1)
    high_ahead = shift(after(high_ahead, low_far), 2, 1)
    late_acts = acts_of(info, low_far, high_far, high_back, low_ahead)
    middle = late_acts.shape[0] // 2
    low_far, high_far = outs_of(late_acts[:middle])
    late_acts, mine_acts = lax.optimization_barrier((late_acts, mine_acts, low_far))[:2]
    high_far = shift(after(high_far, low_back), 2, -1)
    low_far = shift(after(low_far, high_ahead), 2, 1)
    high_back, low_ahead = outs_of(late_acts[middle:])
    low_mine, high_mine = outs_of(mine_acts)
    high_back = after(plus(high_back, high_far).astype(jnp.bfloat16), low_mine)
    low_ahead = after(plus(low_ahead, low_far).astype(jnp.bfloat16), low_mine)
    high_back, low_ahead = shift(high_back, 2, -1), shift(low_ahead, 2, 1)
    low = plus(low_mine, low_back, low_ahead).astype(jnp.bfloat16)
    high = plus(high_mine, high_back, high_ahead).astype(jnp.bfloat16)
    low, high = lax.optimization_barrier((low, high))
    parts = [*jnp.split(low, 2, axis=0), *jnp.split(high, 2, axis=0)]
    for phase in (1, 0):
        moe = plus(parts[0], *(shift(parts[back], phase, -back) for back in range(1, SIDE)))
        if phase > 0:
            parts = jnp.split(moe.astype(jnp.bfloat16), SIDE, axis=0)
    hidden = (resid.astype(jnp.float32) + moe).astype(jnp.bfloat16)
    attn_in = rms_scale(hidden, attn_gain).astype(jnp.bfloat16)
    kv_raw = jnp.dot(attn_in, w_kv, preferred_element_type=jnp.float32)
    latent = rms_scale(kv_raw[:, :KVL], kv_gain)
    rotated = rotate_half(kv_raw[:, KVL:], lengths)
    new_entry = jnp.concatenate([latent, rotated], axis=-1).astype(jnp.bfloat16)
    scores_old = (
        jnp.einsum("thc,tpc->thp", queries, cache, preferred_element_type=jnp.float32) * SCORE_SCALE
    )
    scores_new = (
        jnp.einsum("thc,tc->th", queries, new_entry, preferred_element_type=jnp.float32)
        * SCORE_SCALE
    )
    live_mask = jnp.arange(cache.shape[1], dtype=jnp.int32)[None, None, :] < lengths[:, None, None]
    scores_old = jnp.where(live_mask, scores_old, -jnp.inf)
    peak = jnp.maximum(jnp.max(scores_old, axis=2), scores_new)
    exp_old = jnp.exp(scores_old - peak[:, :, None])
    exp_new = jnp.exp(scores_new - peak)
    denom = jnp.sum(exp_old, axis=2) + exp_new
    probs_old = (exp_old / denom[:, :, None]).astype(jnp.bfloat16)
    probs_new = (exp_new / denom).astype(jnp.bfloat16)
    mixed = jnp.einsum(
        "thp,tpc->thc", probs_old, cache[:, :, :KVL], preferred_element_type=jnp.float32
    )
    mixed = mixed + probs_new.astype(jnp.float32)[:, :, None] * new_entry[:, None, :KVL].astype(
        jnp.float32
    )
    attn_out = mixed.astype(jnp.bfloat16)
    return (hidden, new_entry, attn_out)


def solution(mesh):
    placed = (
        P(("sec", "dev"), None),
        P(),
        P(("sec", "dev"), None),
        P(("sec", "dev"), None),
        P(None, ("sec", "dev")),
        P(None, ("sec", "dev")),
        P(("sec", "dev"), None),
        P(),
        P(),
        P(),
        P(("sec", "dev"), None, None),
        P(("sec", "dev")),
        P(("sec", "dev"), None, None),
    )
    return jax.shard_map(
        on_device,
        mesh=mesh,
        in_specs=placed,
        out_specs=(P(("sec", "dev"), None), P(("sec", "dev"), None), P(("sec", "dev"), None, None)),
        check_vma=False,
    )
```

```python
import functools

import jax
import jax.numpy as jnp
from jax import lax
from jax.experimental import pallas as pl
from jax.experimental.pallas import tpu as pltpu
from jax.sharding import PartitionSpec as P

KVL = 512
EXPERTS = 16
AXES = ("sec", "dev")
SIDE = 4
STRIDE = {"x": 16, "y": 4, "z": 1}
ORDER = (("x", "y", "z"), ("y", "z", "x"))
LANES = 128


norm_eps = 1e-06
SCORE_SCALE = 0.0721687836


def rms_scale(values, gain_vec):
    values = values.astype(jnp.float32)
    return (
        values * lax.rsqrt(jnp.mean(values * values, axis=-1, keepdims=True) + norm_eps) * gain_vec
    )


def rotate_half(rotary, positions):
    half_dim = rotary.shape[-1] // 2
    inv_freq = jnp.exp(
        -jnp.log(10000.0) * jnp.arange(half_dim).astype(jnp.float32) * 2.0 / rotary.shape[-1]
    )
    angles = positions.astype(jnp.float32)[:, None] * inv_freq[None, :]
    lower_half = rotary[:, :half_dim]
    upper_half = rotary[:, half_dim:]
    cosine = jnp.cos(angles)
    sine_val = jnp.sin(angles)
    return jnp.concatenate(
        [lower_half * cosine - upper_half * sine_val, upper_half * cosine + lower_half * sine_val],
        axis=-1,
    )


def shift(values, phase, amount):
    pairs = []
    for sec in range(2):
        stride = STRIDE[ORDER[sec][phase]]
        for dev in range(SIDE**3):
            place = dev // stride % SIDE
            there = dev + ((place + amount) % SIDE - place) * stride
            pairs.append((sec * SIDE**3 + dev, sec * SIDE**3 + there))
    return lax.ppermute(values, AXES, pairs)


def swap_cores(values):
    return lax.ppermute(values, AXES, [(i, (i + SIDE**3) % (2 * SIDE**3)) for i in range(2 * SIDE**3)])


def after(values, *earlier):
    return lax.optimization_barrier((values, *earlier))[0]


def join_body(count, *refs):
    ins, outs, sems = refs[:SIDE], refs[SIDE : SIDE + count], refs[-1]
    each = SIDE // count
    copies = []
    for back in range(SIDE):
        rows = ins[back].shape[0]
        copies.append(
            pltpu.make_async_copy(
                ins[back],
                outs[back // each].at[pl.ds(back % each * rows, rows)],
                sems.at[back],
            )
        )
    for copy in copies:
        copy.start()
    for copy in copies:
        copy.wait()


def join(blocks, count):
    rows, *rest = blocks[0].shape
    hbm = pl.BlockSpec(memory_space=pl.ANY)
    return pl.pallas_call(
        functools.partial(join_body, count),
        out_shape=[jax.ShapeDtypeStruct((SIDE // count * rows, *rest), blocks[0].dtype)] * count,
        in_specs=[hbm] * SIDE,
        out_specs=[hbm] * count,
        scratch_shapes=[pltpu.SemaphoreType.DMA((SIDE,))],
        compiler_params=pltpu.CompilerParams(vmem_limit_bytes=1 << 20),
        name="join",
    )(*blocks)


def front_body(resid_ref, gain_ref, ids_ref, weights_ref, out_ref):
    width = resid_ref.shape[1]
    out_ref[:, :width] = rms_scale(resid_ref[...], gain_ref[...]).astype(jnp.bfloat16)
    lane = lax.broadcasted_iota(jnp.int32, (resid_ref.shape[0], LANES), 1)
    expert = jnp.where(lane < 3 * EXPERTS, lane % EXPERTS, -1)
    dense = jnp.zeros(lane.shape, jnp.float32)
    for number in range(ids_ref.shape[1]):
        hit = ids_ref[:, number : number + 1] == expert
        dense = dense + jnp.where(hit, weights_ref[:, number : number + 1], 0.0)
    high = dense.astype(jnp.bfloat16).astype(jnp.float32)
    rest = dense - high
    middle = rest.astype(jnp.bfloat16).astype(jnp.float32)
    part = jnp.where(lane < EXPERTS, high, jnp.where(lane < 2 * EXPERTS, middle, rest - middle))
    out_ref[:, width:] = part.astype(jnp.bfloat16)


def front(resid, gain_vec, ids, weights):
    rows, width = resid.shape
    vmem = pl.BlockSpec(memory_space=pltpu.VMEM)
    return pl.pallas_call(
        front_body,
        out_shape=jax.ShapeDtypeStruct((rows, width + LANES), jnp.bfloat16),
        in_specs=[vmem] * 4,
        out_specs=vmem,
        compiler_params=pltpu.CompilerParams(vmem_limit_bytes=58 << 20),
        name="front",
    )(resid, gain_vec.reshape(1, width), ids, weights)


def act_body(info_ref, *refs):
    rows, weights, out_ref = refs[:-5], refs[-5:-1], refs[-1]
    depth, wide = weights[0].shape
    held = jnp.concatenate([part[:, depth:] for part in rows], axis=0).astype(jnp.float32)
    lane = lax.broadcasted_iota(jnp.int32, (1, LANES), 1)

    def product(which):
        left = jnp.concatenate([part[:, :depth] for part in rows], axis=0)
        return jnp.dot(left, weights[which][...], preferred_element_type=jnp.float32)

    for which in range(2):
        expert = info_ref[which]
        hit = (lane == expert) | (lane == expert + EXPERTS) | (lane == expert + 2 * EXPERTS)
        weight = jnp.sum(jnp.where(hit, held, 0.0), axis=1, keepdims=True)
        gate = product(which)
        up = product(2 + which)
        act = gate / (1.0 + jnp.exp(-gate)) * up * weight
        out_ref[:, which * wide : (which + 1) * wide] = act.astype(jnp.bfloat16)


def expert_acts(info, rows, weights):
    tokens = sum(part.shape[0] for part in rows)
    depth, wide = weights[0].shape
    vmem = pl.BlockSpec(memory_space=pltpu.VMEM)
    return pl.pallas_call(
        act_body,
        out_shape=jax.ShapeDtypeStruct((tokens, 2 * wide), jnp.bfloat16),
        in_specs=[pl.BlockSpec(memory_space=pltpu.SMEM)] + [vmem] * (len(rows) + 4),
        out_specs=vmem,
        compiler_params=pltpu.CompilerParams(vmem_limit_bytes=18 << 20),
        cost_estimate=pl.CostEstimate(
            flops=8 * tokens * depth * wide, bytes_accessed=1 << 20, transcendentals=0
        ),
        name="expert_acts",
    )(info, *rows, *weights)


def down_body(acts_ref, mine_ref, other_ref, *outs):
    wide = mine_ref.shape[0]
    group = outs[0].shape[0]
    step = 4 * LANES
    for low in range(0, mine_ref.shape[1], step):
        high = low + step
        part = jnp.dot(
            acts_ref[:, :wide], mine_ref[:, low:high], preferred_element_type=jnp.float32
        ) + jnp.dot(acts_ref[:, wide:], other_ref[:, low:high], preferred_element_type=jnp.float32)
        part = part.astype(jnp.bfloat16)
        for number, out in enumerate(outs):
            out[:, low:high] = part[number * group : (number + 1) * group]


def expert_outs(acts, mine, other, count):
    tokens, both = acts.shape
    width = mine.shape[1]
    vmem = pl.BlockSpec(memory_space=pltpu.VMEM)
    return pl.pallas_call(
        down_body,
        out_shape=[jax.ShapeDtypeStruct((tokens // count, width), jnp.bfloat16)] * count,
        in_specs=[vmem] * 3,
        out_specs=[vmem] * count,
        compiler_params=pltpu.CompilerParams(vmem_limit_bytes=18 << 20),
        cost_estimate=pl.CostEstimate(
            flops=2 * tokens * both * width, bytes_accessed=1 << 20, transcendentals=0
        ),
        name="expert_outs",
    )(acts, mine, other)


def plus(first, *others):
    total = first.astype(jnp.float32)
    for other in others:
        total = total + other.astype(jnp.float32)
    return total


def on_device(
    resid,
    ffn_gain,
    expert_ids,
    gate_weights,
    w_gate,
    w_up,
    w_down,
    attn_gain,
    w_kv,
    kv_gain,
    cache,
    lengths,
    queries,
):
    tok_count = resid.shape[0]
    model_width = resid.shape[1]
    sec = lax.axis_index("sec")
    chip_expert = lax.axis_index("dev") // (SIDE**3 // (EXPERTS // 2))
    gate_other = swap_cores(w_gate)
    rows = front(resid, ffn_gain, expert_ids, gate_weights)
    up_other = swap_cores(w_up)
    rows = rows[None]
    (rows,) = join([rows] + [shift(rows, 0, back) for back in range(1, SIDE)], 1)
    got = [rows] + [shift(rows, 1, back) for back in range(1, SIDE)]
    low, high = join(lax.optimization_barrier((got, gate_other, up_other))[0], 2)
    down_other = swap_cores(after(w_down, low))
    low_back, high_ahead = shift(low, 2, 1), shift(high, 2, -1)
    high_back, low_ahead = shift(high, 2, 1), shift(low, 2, -1)

    half = EXPERTS // 2
    info = jnp.stack([chip_expert + sec * half, chip_expert + (1 - sec) * half]).astype(jnp.int32)
    weights = (w_gate, gate_other, w_up, up_other)

    def acts_of(number, *parts):
        return expert_acts(number, [part.reshape(-1, part.shape[-1]) for part in parts], weights)

    def outs_of(acts):
        return expert_outs(acts, w_down, down_other, 2)

    mine_acts = acts_of(info, low, high)
    low_back, high_ahead = lax.optimization_barrier((low_back, high_ahead, mine_acts))[:2]
    low_far, high_far = shift(low_back, 2, 1), shift(high_ahead, 2, -1)
    near_acts = acts_of(info, low_back, high_ahead)
    near_acts, high_back, low_ahead = lax.optimization_barrier((near_acts, high_back, low_ahead))
    low_back, high_ahead = outs_of(near_acts)
    low_back = shift(after(low_back, high_far), 2, -1)
    high_ahead = shift(after(high_ahead, low_far), 2, 1)
    late_acts = acts_of(info, low_far, high_far, high_back, low_ahead)
    middle = late_acts.shape[0] // 2
    low_far, high_far = outs_of(late_acts[:middle])
    late_acts, mine_acts = lax.optimization_barrier((late_acts, mine_acts, low_far))[:2]
    high_far = shift(after(high_far, low_back), 2, -1)
    low_far = shift(after(low_far, high_ahead), 2, 1)
    high_back, low_ahead = outs_of(late_acts[middle:])
    low_mine, high_mine = outs_of(mine_acts)
    high_back = after(plus(high_back, high_far).astype(jnp.bfloat16), low_mine)
    low_ahead = after(plus(low_ahead, low_far).astype(jnp.bfloat16), low_mine)
    high_back, low_ahead = shift(high_back, 2, -1), shift(low_ahead, 2, 1)
    low = plus(low_mine, low_back, low_ahead).astype(jnp.bfloat16)
    high = plus(high_mine, high_back, high_ahead).astype(jnp.bfloat16)
    low, high = lax.optimization_barrier((low, high))
    parts = [*jnp.split(low, 2, axis=0), *jnp.split(high, 2, axis=0)]
    for phase in (1, 0):
        moe = plus(parts[0], *(shift(parts[back], phase, -back) for back in range(1, SIDE)))
        if phase > 0:
            parts = jnp.split(moe.astype(jnp.bfloat16), SIDE, axis=0)
    hidden = (resid.astype(jnp.float32) + moe).astype(jnp.bfloat16)
    attn_in = rms_scale(hidden, attn_gain).astype(jnp.bfloat16)
    kv_raw = jnp.dot(attn_in, w_kv, preferred_element_type=jnp.float32)
    latent = rms_scale(kv_raw[:, :KVL], kv_gain)
    rotated = rotate_half(kv_raw[:, KVL:], lengths)
    new_entry = jnp.concatenate([latent, rotated], axis=-1).astype(jnp.bfloat16)
    scores_old = (
        jnp.einsum("thc,tpc->thp", queries, cache, preferred_element_type=jnp.float32) * SCORE_SCALE
    )
    scores_new = (
        jnp.einsum("thc,tc->th", queries, new_entry, preferred_element_type=jnp.float32)
        * SCORE_SCALE
    )
    live_mask = jnp.arange(cache.shape[1], dtype=jnp.int32)[None, None, :] < lengths[:, None, None]
    scores_old = jnp.where(live_mask, scores_old, -jnp.inf)
    peak = jnp.maximum(jnp.max(scores_old, axis=2), scores_new)
    exp_old = jnp.exp(scores_old - peak[:, :, None])
    exp_new = jnp.exp(scores_new - peak)
    denom = jnp.sum(exp_old, axis=2) + exp_new
    probs_old = (exp_old / denom[:, :, None]).astype(jnp.bfloat16)
    probs_new = (exp_new / denom).astype(jnp.bfloat16)
    mixed = jnp.einsum(
        "thp,tpc->thc", probs_old, cache[:, :, :KVL], preferred_element_type=jnp.float32
    )
    mixed = mixed + probs_new.astype(jnp.float32)[:, :, None] * new_entry[:, None, :KVL].astype(
        jnp.float32
    )
    attn_out = mixed.astype(jnp.bfloat16)
    return (hidden, new_entry, attn_out)


def solution(mesh):
    placed = (
        P(("sec", "dev"), None),
        P(),
        P(("sec", "dev"), None),
        P(("sec", "dev"), None),
        P(None, ("sec", "dev")),
        P(None, ("sec", "dev")),
        P(("sec", "dev"), None),
        P(),
        P(),
        P(),
        P(("sec", "dev"), None, None),
        P(("sec", "dev")),
        P(("sec", "dev"), None, None),
    )
    return jax.shard_map(
        on_device,
        mesh=mesh,
        in_specs=placed,
        out_specs=(P(("sec", "dev"), None), P(("sec", "dev"), None), P(("sec", "dev"), None, None)),
        check_vma=False,
    )
```

```python
import functools

import jax
import jax.numpy as jnp
from jax import lax
from jax.experimental import pallas as pl
from jax.experimental.pallas import tpu as pltpu
from jax.sharding import PartitionSpec as P

KVL = 512
EXPERTS = 16
AXES = ("sec", "dev")
SIDE = 4
STRIDE = {"x": 16, "y": 4, "z": 1}
ORDER = (("y", "x", "z"), ("z", "y", "x"))
LANES = 128


norm_eps = 1e-06
SCORE_SCALE = 0.0721687836


def rms_scale(values, gain_vec):
    values = values.astype(jnp.float32)
    return (
        values * lax.rsqrt(jnp.mean(values * values, axis=-1, keepdims=True) + norm_eps) * gain_vec
    )


def rotate_half(rotary, positions):
    half_dim = rotary.shape[-1] // 2
    inv_freq = jnp.exp(
        -jnp.log(10000.0) * jnp.arange(half_dim).astype(jnp.float32) * 2.0 / rotary.shape[-1]
    )
    angles = positions.astype(jnp.float32)[:, None] * inv_freq[None, :]
    lower_half = rotary[:, :half_dim]
    upper_half = rotary[:, half_dim:]
    cosine = jnp.cos(angles)
    sine_val = jnp.sin(angles)
    return jnp.concatenate(
        [lower_half * cosine - upper_half * sine_val, upper_half * cosine + lower_half * sine_val],
        axis=-1,
    )


def shift(values, phase, amount):
    pairs = []
    for sec in range(2):
        stride = STRIDE[ORDER[sec][phase]]
        for dev in range(SIDE**3):
            place = dev // stride % SIDE
            there = dev + ((place + amount) % SIDE - place) * stride
            pairs.append((sec * SIDE**3 + dev, sec * SIDE**3 + there))
    return lax.ppermute(values, AXES, pairs)


def swap_cores(values):
    return lax.ppermute(values, AXES, [(i, (i + SIDE**3) % (2 * SIDE**3)) for i in range(2 * SIDE**3)])


def after(values, *earlier):
    return lax.optimization_barrier((values, *earlier))[0]


def join_body(count, *refs):
    ins, outs, sems = refs[:SIDE], refs[SIDE : SIDE + count], refs[-1]
    each = SIDE // count
    copies = []
    for back in range(SIDE):
        rows = ins[back].shape[0]
        copies.append(
            pltpu.make_async_copy(
                ins[back],
                outs[back // each].at[pl.ds(back % each * rows, rows)],
                sems.at[back],
            )
        )
    for copy in copies:
        copy.start()
    for copy in copies:
        copy.wait()


def join(blocks, count):
    rows, *rest = blocks[0].shape
    hbm = pl.BlockSpec(memory_space=pl.ANY)
    return pl.pallas_call(
        functools.partial(join_body, count),
        out_shape=[jax.ShapeDtypeStruct((SIDE // count * rows, *rest), blocks[0].dtype)] * count,
        in_specs=[hbm] * SIDE,
        out_specs=[hbm] * count,
        scratch_shapes=[pltpu.SemaphoreType.DMA((SIDE,))],
        compiler_params=pltpu.CompilerParams(vmem_limit_bytes=1 << 20),
        name="join",
    )(*blocks)


def front_body(resid_ref, gain_ref, ids_ref, weights_ref, out_ref):
    width = resid_ref.shape[1]
    out_ref[:, :width] = rms_scale(resid_ref[...], gain_ref[...]).astype(jnp.bfloat16)
    lane = lax.broadcasted_iota(jnp.int32, (resid_ref.shape[0], LANES), 1)
    expert = jnp.where(lane < 3 * EXPERTS, lane % EXPERTS, -1)
    dense = jnp.zeros(lane.shape, jnp.float32)
    for number in range(ids_ref.shape[1]):
        hit = ids_ref[:, number : number + 1] == expert
        dense = dense + jnp.where(hit, weights_ref[:, number : number + 1], 0.0)
    high = dense.astype(jnp.bfloat16).astype(jnp.float32)
    rest = dense - high
    middle = rest.astype(jnp.bfloat16).astype(jnp.float32)
    part = jnp.where(lane < EXPERTS, high, jnp.where(lane < 2 * EXPERTS, middle, rest - middle))
    out_ref[:, width:] = part.astype(jnp.bfloat16)


def front(resid, gain_vec, ids, weights):
    rows, width = resid.shape
    vmem = pl.BlockSpec(memory_space=pltpu.VMEM)
    return pl.pallas_call(
        front_body,
        out_shape=jax.ShapeDtypeStruct((rows, width + LANES), jnp.bfloat16),
        in_specs=[vmem] * 4,
        out_specs=vmem,
        compiler_params=pltpu.CompilerParams(vmem_limit_bytes=58 << 20),
        name="front",
    )(resid, gain_vec.reshape(1, width), ids, weights)


def act_body(info_ref, *refs):
    rows, weights, out_ref = refs[:-5], refs[-5:-1], refs[-1]
    depth, wide = weights[0].shape
    held = jnp.concatenate([part[:, depth:] for part in rows], axis=0).astype(jnp.float32)
    lane = lax.broadcasted_iota(jnp.int32, (1, LANES), 1)

    def product(which):
        left = jnp.concatenate([part[:, :depth] for part in rows], axis=0)
        return jnp.dot(left, weights[which][...], preferred_element_type=jnp.float32)

    for which in range(2):
        expert = info_ref[which]
        hit = (lane == expert) | (lane == expert + EXPERTS) | (lane == expert + 2 * EXPERTS)
        weight = jnp.sum(jnp.where(hit, held, 0.0), axis=1, keepdims=True)
        gate = product(which)
        up = product(2 + which)
        act = gate / (1.0 + jnp.exp(-gate)) * up * weight
        out_ref[:, which * wide : (which + 1) * wide] = act.astype(jnp.bfloat16)


def expert_acts(info, rows, weights):
    tokens = sum(part.shape[0] for part in rows)
    depth, wide = weights[0].shape
    vmem = pl.BlockSpec(memory_space=pltpu.VMEM)
    return pl.pallas_call(
        act_body,
        out_shape=jax.ShapeDtypeStruct((tokens, 2 * wide), jnp.bfloat16),
        in_specs=[pl.BlockSpec(memory_space=pltpu.SMEM)] + [vmem] * (len(rows) + 4),
        out_specs=vmem,
        compiler_params=pltpu.CompilerParams(vmem_limit_bytes=18 << 20),
        cost_estimate=pl.CostEstimate(
            flops=8 * tokens * depth * wide, bytes_accessed=1 << 20, transcendentals=0
        ),
        name="expert_acts",
    )(info, *rows, *weights)


def down_body(acts_ref, mine_ref, other_ref, *outs):
    wide = mine_ref.shape[0]
    group = outs[0].shape[0]
    step = 4 * LANES
    for low in range(0, mine_ref.shape[1], step):
        high = low + step
        part = jnp.dot(
            acts_ref[:, :wide], mine_ref[:, low:high], preferred_element_type=jnp.float32
        ) + jnp.dot(acts_ref[:, wide:], other_ref[:, low:high], preferred_element_type=jnp.float32)
        part = part.astype(jnp.bfloat16)
        for number, out in enumerate(outs):
            out[:, low:high] = part[number * group : (number + 1) * group]


def expert_outs(acts, mine, other, count):
    tokens, both = acts.shape
    width = mine.shape[1]
    vmem = pl.BlockSpec(memory_space=pltpu.VMEM)
    return pl.pallas_call(
        down_body,
        out_shape=[jax.ShapeDtypeStruct((tokens // count, width), jnp.bfloat16)] * count,
        in_specs=[vmem] * 3,
        out_specs=[vmem] * count,
        compiler_params=pltpu.CompilerParams(vmem_limit_bytes=18 << 20),
        cost_estimate=pl.CostEstimate(
            flops=2 * tokens * both * width, bytes_accessed=1 << 20, transcendentals=0
        ),
        name="expert_outs",
    )(acts, mine, other)


def plus(first, *others):
    total = first.astype(jnp.float32)
    for other in others:
        total = total + other.astype(jnp.float32)
    return total


def on_device(
    resid,
    ffn_gain,
    expert_ids,
    gate_weights,
    w_gate,
    w_up,
    w_down,
    attn_gain,
    w_kv,
    kv_gain,
    cache,
    lengths,
    queries,
):
    tok_count = resid.shape[0]
    model_width = resid.shape[1]
    sec = lax.axis_index("sec")
    chip_expert = lax.axis_index("dev") // (SIDE**3 // (EXPERTS // 2))
    gate_other = swap_cores(w_gate)
    rows = front(resid, ffn_gain, expert_ids, gate_weights)
    up_other = swap_cores(w_up)
    rows = rows[None]
    (rows,) = join([rows] + [shift(rows, 0, back) for back in range(1, SIDE)], 1)
    got = [rows] + [shift(rows, 1, back) for back in range(1, SIDE)]
    low, high = join(lax.optimization_barrier((got, gate_other, up_other))[0], 2)
    down_other = swap_cores(after(w_down, low))
    low_back, high_ahead = shift(low, 2, 1), shift(high, 2, -1)
    high_back, low_ahead = shift(high, 2, 1), shift(low, 2, -1)

    half = EXPERTS // 2
    info = jnp.stack([chip_expert + sec * half, chip_expert + (1 - sec) * half]).astype(jnp.int32)
    weights = (w_gate, gate_other, w_up, up_other)

    def acts_of(number, *parts):
        return expert_acts(number, [part.reshape(-1, part.shape[-1]) for part in parts], weights)

    def outs_of(acts):
        return expert_outs(acts, w_down, down_other, 2)

    mine_acts = acts_of(info, low, high)
    low_back, high_ahead = lax.optimization_barrier((low_back, high_ahead, mine_acts))[:2]
    low_far, high_far = shift(low_back, 2, 1), shift(high_ahead, 2, -1)
    near_acts = acts_of(info, low_back, high_ahead)
    near_acts, high_back, low_ahead = lax.optimization_barrier((near_acts, high_back, low_ahead))
    low_back, high_ahead = outs_of(near_acts)
    low_back = shift(after(low_back, high_far), 2, -1)
    high_ahead = shift(after(high_ahead, low_far), 2, 1)
    late_acts = acts_of(info, low_far, high_far, high_back, low_ahead)
    middle = late_acts.shape[0] // 2
    low_far, high_far = outs_of(late_acts[:middle])
    late_acts, mine_acts = lax.optimization_barrier((late_acts, mine_acts, low_far))[:2]
    high_far = shift(after(high_far, low_back), 2, -1)
    low_far = shift(after(low_far, high_ahead), 2, 1)
    high_back, low_ahead = outs_of(late_acts[middle:])
    low_mine, high_mine = outs_of(mine_acts)
    high_back = after(plus(high_back, high_far).astype(jnp.bfloat16), low_mine)
    low_ahead = after(plus(low_ahead, low_far).astype(jnp.bfloat16), low_mine)
    high_back, low_ahead = shift(high_back, 2, -1), shift(low_ahead, 2, 1)
    low = plus(low_mine, low_back, low_ahead).astype(jnp.bfloat16)
    high = plus(high_mine, high_back, high_ahead).astype(jnp.bfloat16)
    low, high = lax.optimization_barrier((low, high))
    parts = [*jnp.split(low, 2, axis=0), *jnp.split(high, 2, axis=0)]
    for phase in (1, 0):
        moe = plus(parts[0], *(shift(parts[back], phase, -back) for back in range(1, SIDE)))
        if phase > 0:
            parts = jnp.split(moe.astype(jnp.bfloat16), SIDE, axis=0)
    hidden = (resid.astype(jnp.float32) + moe).astype(jnp.bfloat16)
    attn_in = rms_scale(hidden, attn_gain).astype(jnp.bfloat16)
    kv_raw = jnp.dot(attn_in, w_kv, preferred_element_type=jnp.float32)
    latent = rms_scale(kv_raw[:, :KVL], kv_gain)
    rotated = rotate_half(kv_raw[:, KVL:], lengths)
    new_entry = jnp.concatenate([latent, rotated], axis=-1).astype(jnp.bfloat16)
    scores_old = (
        jnp.einsum("thc,tpc->thp", queries, cache, preferred_element_type=jnp.float32) * SCORE_SCALE
    )
    scores_new = (
        jnp.einsum("thc,tc->th", queries, new_entry, preferred_element_type=jnp.float32)
        * SCORE_SCALE
    )
    live_mask = jnp.arange(cache.shape[1], dtype=jnp.int32)[None, None, :] < lengths[:, None, None]
    scores_old = jnp.where(live_mask, scores_old, -jnp.inf)
    peak = jnp.maximum(jnp.max(scores_old, axis=2), scores_new)
    exp_old = jnp.exp(scores_old - peak[:, :, None])
    exp_new = jnp.exp(scores_new - peak)
    denom = jnp.sum(exp_old, axis=2) + exp_new
    probs_old = (exp_old / denom[:, :, None]).astype(jnp.bfloat16)
    probs_new = (exp_new / denom).astype(jnp.bfloat16)
    mixed = jnp.einsum(
        "thp,tpc->thc", probs_old, cache[:, :, :KVL], preferred_element_type=jnp.float32
    )
    mixed = mixed + probs_new.astype(jnp.float32)[:, :, None] * new_entry[:, None, :KVL].astype(
        jnp.float32
    )
    attn_out = mixed.astype(jnp.bfloat16)
    return (hidden, new_entry, attn_out)


def solution(mesh):
    placed = (
        P(("sec", "dev"), None),
        P(),
        P(("sec", "dev"), None),
        P(("sec", "dev"), None),
        P(None, ("sec", "dev")),
        P(None, ("sec", "dev")),
        P(("sec", "dev"), None),
        P(),
        P(),
        P(),
        P(("sec", "dev"), None, None),
        P(("sec", "dev")),
        P(("sec", "dev"), None, None),
    )
    return jax.shard_map(
        on_device,
        mesh=mesh,
        in_specs=placed,
        out_specs=(P(("sec", "dev"), None), P(("sec", "dev"), None), P(("sec", "dev"), None, None)),
        check_vma=False,
    )
```

```python
import functools

import jax
import jax.numpy as jnp
from jax import lax
from jax.experimental import pallas as pl
from jax.experimental.pallas import tpu as pltpu
from jax.sharding import PartitionSpec as P

KVL = 512
EXPERTS = 16
AXES = ("sec", "dev")
SIDE = 4
STRIDE = {"x": 16, "y": 4, "z": 1}
ORDER = (("z", "x", "y"), ("y", "z", "x"))
LANES = 128


norm_eps = 1e-06
SCORE_SCALE = 0.0721687836


def rms_scale(values, gain_vec):
    values = values.astype(jnp.float32)
    return (
        values * lax.rsqrt(jnp.mean(values * values, axis=-1, keepdims=True) + norm_eps) * gain_vec
    )


def rotate_half(rotary, positions):
    half_dim = rotary.shape[-1] // 2
    inv_freq = jnp.exp(
        -jnp.log(10000.0) * jnp.arange(half_dim).astype(jnp.float32) * 2.0 / rotary.shape[-1]
    )
    angles = positions.astype(jnp.float32)[:, None] * inv_freq[None, :]
    lower_half = rotary[:, :half_dim]
    upper_half = rotary[:, half_dim:]
    cosine = jnp.cos(angles)
    sine_val = jnp.sin(angles)
    return jnp.concatenate(
        [lower_half * cosine - upper_half * sine_val, upper_half * cosine + lower_half * sine_val],
        axis=-1,
    )


def shift(values, phase, amount):
    pairs = []
    for sec in range(2):
        stride = STRIDE[ORDER[sec][phase]]
        for dev in range(SIDE**3):
            place = dev // stride % SIDE
            there = dev + ((place + amount) % SIDE - place) * stride
            pairs.append((sec * SIDE**3 + dev, sec * SIDE**3 + there))
    return lax.ppermute(values, AXES, pairs)


def swap_cores(values):
    return lax.ppermute(values, AXES, [(i, (i + SIDE**3) % (2 * SIDE**3)) for i in range(2 * SIDE**3)])


def after(values, *earlier):
    return lax.optimization_barrier((values, *earlier))[0]


def join_body(count, *refs):
    ins, outs, sems = refs[:SIDE], refs[SIDE : SIDE + count], refs[-1]
    each = SIDE // count
    copies = []
    for back in range(SIDE):
        rows = ins[back].shape[0]
        copies.append(
            pltpu.make_async_copy(
                ins[back],
                outs[back // each].at[pl.ds(back % each * rows, rows)],
                sems.at[back],
            )
        )
    for copy in copies:
        copy.start()
    for copy in copies:
        copy.wait()


def join(blocks, count):
    rows, *rest = blocks[0].shape
    hbm = pl.BlockSpec(memory_space=pl.ANY)
    return pl.pallas_call(
        functools.partial(join_body, count),
        out_shape=[jax.ShapeDtypeStruct((SIDE // count * rows, *rest), blocks[0].dtype)] * count,
        in_specs=[hbm] * SIDE,
        out_specs=[hbm] * count,
        scratch_shapes=[pltpu.SemaphoreType.DMA((SIDE,))],
        compiler_params=pltpu.CompilerParams(vmem_limit_bytes=1 << 20),
        name="join",
    )(*blocks)


def front_body(resid_ref, gain_ref, ids_ref, weights_ref, out_ref):
    width = resid_ref.shape[1]
    out_ref[:, :width] = rms_scale(resid_ref[...], gain_ref[...]).astype(jnp.bfloat16)
    lane = lax.broadcasted_iota(jnp.int32, (resid_ref.shape[0], LANES), 1)
    expert = jnp.where(lane < 3 * EXPERTS, lane % EXPERTS, -1)
    dense = jnp.zeros(lane.shape, jnp.float32)
    for number in range(ids_ref.shape[1]):
        hit = ids_ref[:, number : number + 1] == expert
        dense = dense + jnp.where(hit, weights_ref[:, number : number + 1], 0.0)
    high = dense.astype(jnp.bfloat16).astype(jnp.float32)
    rest = dense - high
    middle = rest.astype(jnp.bfloat16).astype(jnp.float32)
    part = jnp.where(lane < EXPERTS, high, jnp.where(lane < 2 * EXPERTS, middle, rest - middle))
    out_ref[:, width:] = part.astype(jnp.bfloat16)


def front(resid, gain_vec, ids, weights):
    rows, width = resid.shape
    vmem = pl.BlockSpec(memory_space=pltpu.VMEM)
    return pl.pallas_call(
        front_body,
        out_shape=jax.ShapeDtypeStruct((rows, width + LANES), jnp.bfloat16),
        in_specs=[vmem] * 4,
        out_specs=vmem,
        compiler_params=pltpu.CompilerParams(vmem_limit_bytes=58 << 20),
        name="front",
    )(resid, gain_vec.reshape(1, width), ids, weights)


def act_body(info_ref, *refs):
    rows, weights, out_ref = refs[:-5], refs[-5:-1], refs[-1]
    depth, wide = weights[0].shape
    held = jnp.concatenate([part[:, depth:] for part in rows], axis=0).astype(jnp.float32)
    lane = lax.broadcasted_iota(jnp.int32, (1, LANES), 1)

    def product(which):
        left = jnp.concatenate([part[:, :depth] for part in rows], axis=0)
        return jnp.dot(left, weights[which][...], preferred_element_type=jnp.float32)

    for which in range(2):
        expert = info_ref[which]
        hit = (lane == expert) | (lane == expert + EXPERTS) | (lane == expert + 2 * EXPERTS)
        weight = jnp.sum(jnp.where(hit, held, 0.0), axis=1, keepdims=True)
        gate = product(which)
        up = product(2 + which)
        act = gate / (1.0 + jnp.exp(-gate)) * up * weight
        out_ref[:, which * wide : (which + 1) * wide] = act.astype(jnp.bfloat16)


def expert_acts(info, rows, weights):
    tokens = sum(part.shape[0] for part in rows)
    depth, wide = weights[0].shape
    vmem = pl.BlockSpec(memory_space=pltpu.VMEM)
    return pl.pallas_call(
        act_body,
        out_shape=jax.ShapeDtypeStruct((tokens, 2 * wide), jnp.bfloat16),
        in_specs=[pl.BlockSpec(memory_space=pltpu.SMEM)] + [vmem] * (len(rows) + 4),
        out_specs=vmem,
        compiler_params=pltpu.CompilerParams(vmem_limit_bytes=18 << 20),
        cost_estimate=pl.CostEstimate(
            flops=8 * tokens * depth * wide, bytes_accessed=1 << 20, transcendentals=0
        ),
        name="expert_acts",
    )(info, *rows, *weights)


def down_body(acts_ref, mine_ref, other_ref, *outs):
    wide = mine_ref.shape[0]
    group = outs[0].shape[0]
    step = 4 * LANES
    for low in range(0, mine_ref.shape[1], step):
        high = low + step
        part = jnp.dot(
            acts_ref[:, :wide], mine_ref[:, low:high], preferred_element_type=jnp.float32
        ) + jnp.dot(acts_ref[:, wide:], other_ref[:, low:high], preferred_element_type=jnp.float32)
        part = part.astype(jnp.bfloat16)
        for number, out in enumerate(outs):
            out[:, low:high] = part[number * group : (number + 1) * group]


def expert_outs(acts, mine, other, count):
    tokens, both = acts.shape
    width = mine.shape[1]
    vmem = pl.BlockSpec(memory_space=pltpu.VMEM)
    return pl.pallas_call(
        down_body,
        out_shape=[jax.ShapeDtypeStruct((tokens // count, width), jnp.bfloat16)] * count,
        in_specs=[vmem] * 3,
        out_specs=[vmem] * count,
        compiler_params=pltpu.CompilerParams(vmem_limit_bytes=18 << 20),
        cost_estimate=pl.CostEstimate(
            flops=2 * tokens * both * width, bytes_accessed=1 << 20, transcendentals=0
        ),
        name="expert_outs",
    )(acts, mine, other)


def plus(first, *others):
    total = first.astype(jnp.float32)
    for other in others:
        total = total + other.astype(jnp.float32)
    return total


def on_device(
    resid,
    ffn_gain,
    expert_ids,
    gate_weights,
    w_gate,
    w_up,
    w_down,
    attn_gain,
    w_kv,
    kv_gain,
    cache,
    lengths,
    queries,
):
    tok_count = resid.shape[0]
    model_width = resid.shape[1]
    sec = lax.axis_index("sec")
    chip_expert = lax.axis_index("dev") // (SIDE**3 // (EXPERTS // 2))
    gate_other = swap_cores(w_gate)
    rows = front(resid, ffn_gain, expert_ids, gate_weights)
    up_other = swap_cores(w_up)
    rows = rows[None]
    (rows,) = join([rows] + [shift(rows, 0, back) for back in range(1, SIDE)], 1)
    got = [rows] + [shift(rows, 1, back) for back in range(1, SIDE)]
    low, high = join(lax.optimization_barrier((got, gate_other, up_other))[0], 2)
    down_other = swap_cores(after(w_down, low))
    low_back, high_ahead = shift(low, 2, 1), shift(high, 2, -1)
    high_back, low_ahead = shift(high, 2, 1), shift(low, 2, -1)

    half = EXPERTS // 2
    info = jnp.stack([chip_expert + sec * half, chip_expert + (1 - sec) * half]).astype(jnp.int32)
    weights = (w_gate, gate_other, w_up, up_other)

    def acts_of(number, *parts):
        return expert_acts(number, [part.reshape(-1, part.shape[-1]) for part in parts], weights)

    def outs_of(acts):
        return expert_outs(acts, w_down, down_other, 2)

    mine_acts = acts_of(info, low, high)
    low_back, high_ahead = lax.optimization_barrier((low_back, high_ahead, mine_acts))[:2]
    low_far, high_far = shift(low_back, 2, 1), shift(high_ahead, 2, -1)
    near_acts = acts_of(info, low_back, high_ahead)
    near_acts, high_back, low_ahead = lax.optimization_barrier((near_acts, high_back, low_ahead))
    low_back, high_ahead = outs_of(near_acts)
    low_back = shift(after(low_back, high_far), 2, -1)
    high_ahead = shift(after(high_ahead, low_far), 2, 1)
    late_acts = acts_of(info, low_far, high_far, high_back, low_ahead)
    middle = late_acts.shape[0] // 2
    low_far, high_far = outs_of(late_acts[:middle])
    late_acts, mine_acts = lax.optimization_barrier((late_acts, mine_acts, low_far))[:2]
    high_far = shift(after(high_far, low_back), 2, -1)
    low_far = shift(after(low_far, high_ahead), 2, 1)
    high_back, low_ahead = outs_of(late_acts[middle:])
    low_mine, high_mine = outs_of(mine_acts)
    high_back = after(plus(high_back, high_far).astype(jnp.bfloat16), low_mine)
    low_ahead = after(plus(low_ahead, low_far).astype(jnp.bfloat16), low_mine)
    high_back, low_ahead = shift(high_back, 2, -1), shift(low_ahead, 2, 1)
    low = plus(low_mine, low_back, low_ahead).astype(jnp.bfloat16)
    high = plus(high_mine, high_back, high_ahead).astype(jnp.bfloat16)
    low, high = lax.optimization_barrier((low, high))
    parts = [*jnp.split(low, 2, axis=0), *jnp.split(high, 2, axis=0)]
    for phase in (1, 0):
        moe = plus(parts[0], *(shift(parts[back], phase, -back) for back in range(1, SIDE)))
        if phase > 0:
            parts = jnp.split(moe.astype(jnp.bfloat16), SIDE, axis=0)
    hidden = (resid.astype(jnp.float32) + moe).astype(jnp.bfloat16)
    attn_in = rms_scale(hidden, attn_gain).astype(jnp.bfloat16)
    kv_raw = jnp.dot(attn_in, w_kv, preferred_element_type=jnp.float32)
    latent = rms_scale(kv_raw[:, :KVL], kv_gain)
    rotated = rotate_half(kv_raw[:, KVL:], lengths)
    new_entry = jnp.concatenate([latent, rotated], axis=-1).astype(jnp.bfloat16)
    scores_old = (
        jnp.einsum("thc,tpc->thp", queries, cache, preferred_element_type=jnp.float32) * SCORE_SCALE
    )
    scores_new = (
        jnp.einsum("thc,tc->th", queries, new_entry, preferred_element_type=jnp.float32)
        * SCORE_SCALE
    )
    live_mask = jnp.arange(cache.shape[1], dtype=jnp.int32)[None, None, :] < lengths[:, None, None]
    scores_old = jnp.where(live_mask, scores_old, -jnp.inf)
    peak = jnp.maximum(jnp.max(scores_old, axis=2), scores_new)
    exp_old = jnp.exp(scores_old - peak[:, :, None])
    exp_new = jnp.exp(scores_new - peak)
    denom = jnp.sum(exp_old, axis=2) + exp_new
    probs_old = (exp_old / denom[:, :, None]).astype(jnp.bfloat16)
    probs_new = (exp_new / denom).astype(jnp.bfloat16)
    mixed = jnp.einsum(
        "thp,tpc->thc", probs_old, cache[:, :, :KVL], preferred_element_type=jnp.float32
    )
    mixed = mixed + probs_new.astype(jnp.float32)[:, :, None] * new_entry[:, None, :KVL].astype(
        jnp.float32
    )
    attn_out = mixed.astype(jnp.bfloat16)
    return (hidden, new_entry, attn_out)


def solution(mesh):
    placed = (
        P(("sec", "dev"), None),
        P(),
        P(("sec", "dev"), None),
        P(("sec", "dev"), None),
        P(None, ("sec", "dev")),
        P(None, ("sec", "dev")),
        P(("sec", "dev"), None),
        P(),
        P(),
        P(),
        P(("sec", "dev"), None, None),
        P(("sec", "dev")),
        P(("sec", "dev"), None, None),
    )
    return jax.shard_map(
        on_device,
        mesh=mesh,
        in_specs=placed,
        out_specs=(P(("sec", "dev"), None), P(("sec", "dev"), None), P(("sec", "dev"), None, None)),
        check_vma=False,
    )
```

```python
import functools

import jax
import jax.numpy as jnp
from jax import lax
from jax.experimental import pallas as pl
from jax.experimental.pallas import tpu as pltpu
from jax.sharding import PartitionSpec as P

KVL = 512
EXPERTS = 16
AXES = ("sec", "dev")
SIDE = 4
STRIDE = {"x": 16, "y": 4, "z": 1}
ORDER = (("z", "x", "y"), ("y", "z", "x"))
LANES = 128


norm_eps = 1e-06
SCORE_SCALE = 0.0721687836


def rms_scale(values, gain_vec):
    values = values.astype(jnp.float32)
    return (
        values * lax.rsqrt(jnp.mean(values * values, axis=-1, keepdims=True) + norm_eps) * gain_vec
    )


def rotate_half(rotary, positions):
    half_dim = rotary.shape[-1] // 2
    inv_freq = jnp.exp(
        -jnp.log(10000.0) * jnp.arange(half_dim).astype(jnp.float32) * 2.0 / rotary.shape[-1]
    )
    angles = positions.astype(jnp.float32)[:, None] * inv_freq[None, :]
    lower_half = rotary[:, :half_dim]
    upper_half = rotary[:, half_dim:]
    cosine = jnp.cos(angles)
    sine_val = jnp.sin(angles)
    return jnp.concatenate(
        [lower_half * cosine - upper_half * sine_val, upper_half * cosine + lower_half * sine_val],
        axis=-1,
    )


def shift(values, phase, amount):
    pairs = []
    for sec in range(2):
        stride = STRIDE[ORDER[sec][phase]]
        for dev in range(SIDE**3):
            place = dev // stride % SIDE
            there = dev + ((place + amount) % SIDE - place) * stride
            pairs.append((sec * SIDE**3 + dev, sec * SIDE**3 + there))
    return lax.ppermute(values, AXES, pairs)


def swap_cores(values):
    return lax.ppermute(values, AXES, [(i, (i + SIDE**3) % (2 * SIDE**3)) for i in range(2 * SIDE**3)])


def after(values, *earlier):
    return lax.optimization_barrier((values, *earlier))[0]


def join_body(count, *refs):
    ins, outs, sems = refs[:SIDE], refs[SIDE : SIDE + count], refs[-1]
    each = SIDE // count
    copies = []
    for back in range(SIDE):
        rows = ins[back].shape[0]
        copies.append(
            pltpu.make_async_copy(
                ins[back],
                outs[back // each].at[pl.ds(back % each * rows, rows)],
                sems.at[back],
            )
        )
    for copy in copies:
        copy.start()
    for copy in copies:
        copy.wait()


def join(blocks, count):
    rows, *rest = blocks[0].shape
    hbm = pl.BlockSpec(memory_space=pl.ANY)
    return pl.pallas_call(
        functools.partial(join_body, count),
        out_shape=[jax.ShapeDtypeStruct((SIDE // count * rows, *rest), blocks[0].dtype)] * count,
        in_specs=[hbm] * SIDE,
        out_specs=[hbm] * count,
        scratch_shapes=[pltpu.SemaphoreType.DMA((SIDE,))],
        compiler_params=pltpu.CompilerParams(vmem_limit_bytes=1 << 20),
        name="join",
    )(*blocks)


def front_body(resid_ref, gain_ref, ids_ref, weights_ref, out_ref):
    width = resid_ref.shape[1]
    out_ref[:, :width] = rms_scale(resid_ref[...], gain_ref[...]).astype(jnp.bfloat16)
    lane = lax.broadcasted_iota(jnp.int32, (resid_ref.shape[0], LANES), 1)
    expert = jnp.where(lane < 3 * EXPERTS, lane % EXPERTS, -1)
    dense = jnp.zeros(lane.shape, jnp.float32)
    for number in range(ids_ref.shape[1]):
        hit = ids_ref[:, number : number + 1] == expert
        dense = dense + jnp.where(hit, weights_ref[:, number : number + 1], 0.0)
    high = dense.astype(jnp.bfloat16).astype(jnp.float32)
    rest = dense - high
    middle = rest.astype(jnp.bfloat16).astype(jnp.float32)
    part = jnp.where(lane < EXPERTS, high, jnp.where(lane < 2 * EXPERTS, middle, rest - middle))
    out_ref[:, width:] = part.astype(jnp.bfloat16)


def front(resid, gain_vec, ids, weights):
    rows, width = resid.shape
    vmem = pl.BlockSpec(memory_space=pltpu.VMEM)
    return pl.pallas_call(
        front_body,
        out_shape=jax.ShapeDtypeStruct((rows, width + LANES), jnp.bfloat16),
        in_specs=[vmem] * 4,
        out_specs=vmem,
        compiler_params=pltpu.CompilerParams(vmem_limit_bytes=58 << 20),
        name="front",
    )(resid, gain_vec.reshape(1, width), ids, weights)


def act_body(info_ref, *refs):
    rows, weights, out_ref = refs[:-5], refs[-5:-1], refs[-1]
    depth, wide = weights[0].shape
    held = jnp.concatenate([part[:, depth:] for part in rows], axis=0).astype(jnp.float32)
    lane = lax.broadcasted_iota(jnp.int32, (1, LANES), 1)

    def product(which):
        left = jnp.concatenate([part[:, :depth] for part in rows], axis=0)
        return jnp.dot(left, weights[which][...], preferred_element_type=jnp.float32)

    for which in range(2):
        expert = info_ref[which]
        hit = (lane == expert) | (lane == expert + EXPERTS) | (lane == expert + 2 * EXPERTS)
        weight = jnp.sum(jnp.where(hit, held, 0.0), axis=1, keepdims=True)
        gate = product(which)
        up = product(2 + which)
        act = gate / (1.0 + jnp.exp(-gate)) * up * weight
        out_ref[:, which * wide : (which + 1) * wide] = act.astype(jnp.bfloat16)


def expert_acts(info, rows, weights):
    tokens = sum(part.shape[0] for part in rows)
    depth, wide = weights[0].shape
    vmem = pl.BlockSpec(memory_space=pltpu.VMEM)
    return pl.pallas_call(
        act_body,
        out_shape=jax.ShapeDtypeStruct((tokens, 2 * wide), jnp.bfloat16),
        in_specs=[pl.BlockSpec(memory_space=pltpu.SMEM)] + [vmem] * (len(rows) + 4),
        out_specs=vmem,
        compiler_params=pltpu.CompilerParams(vmem_limit_bytes=18 << 20),
        cost_estimate=pl.CostEstimate(
            flops=8 * tokens * depth * wide, bytes_accessed=1 << 20, transcendentals=0
        ),
        name="expert_acts",
    )(info, *rows, *weights)


def down_body(acts_ref, mine_ref, other_ref, *outs):
    wide = mine_ref.shape[0]
    group = outs[0].shape[0]
    step = 4 * LANES
    for low in range(0, mine_ref.shape[1], step):
        high = low + step
        part = jnp.dot(
            acts_ref[:, :wide], mine_ref[:, low:high], preferred_element_type=jnp.float32
        ) + jnp.dot(acts_ref[:, wide:], other_ref[:, low:high], preferred_element_type=jnp.float32)
        part = part.astype(jnp.bfloat16)
        for number, out in enumerate(outs):
            out[:, low:high] = part[number * group : (number + 1) * group]


def expert_outs(acts, mine, other, count):
    tokens, both = acts.shape
    width = mine.shape[1]
    vmem = pl.BlockSpec(memory_space=pltpu.VMEM)
    return pl.pallas_call(
        down_body,
        out_shape=[jax.ShapeDtypeStruct((tokens // count, width), jnp.bfloat16)] * count,
        in_specs=[vmem] * 3,
        out_specs=[vmem] * count,
        compiler_params=pltpu.CompilerParams(vmem_limit_bytes=18 << 20),
        cost_estimate=pl.CostEstimate(
            flops=2 * tokens * both * width, bytes_accessed=1 << 20, transcendentals=0
        ),
        name="expert_outs",
    )(acts, mine, other)


def plus(first, *others):
    total = first.astype(jnp.float32)
    for other in others:
        total = total + other.astype(jnp.float32)
    return total


def on_device(
    resid,
    ffn_gain,
    expert_ids,
    gate_weights,
    w_gate,
    w_up,
    w_down,
    attn_gain,
    w_kv,
    kv_gain,
    cache,
    lengths,
    queries,
):
    tok_count = resid.shape[0]
    model_width = resid.shape[1]
    sec = lax.axis_index("sec")
    chip_expert = lax.axis_index("dev") // (SIDE**3 // (EXPERTS // 2))
    gate_other = swap_cores(w_gate)
    rows = front(resid, ffn_gain, expert_ids, gate_weights)
    up_other = swap_cores(w_up)
    rows = rows[None]
    one, three, two = (shift(rows, 0, back) for back in (1, 3, 2))
    (rows,) = join([rows, one, two, three], 1)
    one, three, two = (shift(rows, 1, back) for back in (1, 3, 2))
    got = [rows, one, two, three]
    low, high = join(lax.optimization_barrier((got, gate_other, up_other))[0], 2)
    down_other = swap_cores(after(w_down, low))
    low_back, high_ahead = shift(low, 2, 1), shift(high, 2, -1)
    high_back, low_ahead = shift(high, 2, 1), shift(low, 2, -1)

    half = EXPERTS // 2
    info = jnp.stack([chip_expert + sec * half, chip_expert + (1 - sec) * half]).astype(jnp.int32)
    weights = (w_gate, gate_other, w_up, up_other)

    def acts_of(number, *parts):
        return expert_acts(number, [part.reshape(-1, part.shape[-1]) for part in parts], weights)

    def outs_of(acts):
        return expert_outs(acts, w_down, down_other, 2)

    mine_acts = acts_of(info, low, high)
    low_back, high_ahead = lax.optimization_barrier((low_back, high_ahead, mine_acts))[:2]
    low_far, high_far = shift(low_back, 2, 1), shift(high_ahead, 2, -1)
    near_acts = acts_of(info, low_back, high_ahead)
    near_acts, high_back, low_ahead = lax.optimization_barrier((near_acts, high_back, low_ahead))
    low_back, high_ahead = outs_of(near_acts)
    low_back = shift(after(low_back, high_far), 2, -1)
    high_ahead = shift(after(high_ahead, low_far), 2, 1)
    late_acts = acts_of(info, low_far, high_far, high_back, low_ahead)
    middle = late_acts.shape[0] // 2
    low_far, high_far = outs_of(late_acts[:middle])
    late_acts, mine_acts = lax.optimization_barrier((late_acts, mine_acts, low_far))[:2]
    high_far = shift(after(high_far, low_back), 2, -1)
    low_far = shift(after(low_far, high_ahead), 2, 1)
    high_back, low_ahead = outs_of(late_acts[middle:])
    low_mine, high_mine = outs_of(mine_acts)
    high_back = after(plus(high_back, high_far).astype(jnp.bfloat16), low_mine)
    low_ahead = after(plus(low_ahead, low_far).astype(jnp.bfloat16), low_mine)
    high_back, low_ahead = shift(high_back, 2, -1), shift(low_ahead, 2, 1)
    low = plus(low_mine, low_back, low_ahead).astype(jnp.bfloat16)
    high = plus(high_mine, high_back, high_ahead).astype(jnp.bfloat16)
    low, high = lax.optimization_barrier((low, high))
    parts = [*jnp.split(low, 2, axis=0), *jnp.split(high, 2, axis=0)]
    for phase in (1, 0):
        moe = plus(parts[0], *(shift(parts[back], phase, -back) for back in (1, 3, 2)))
        if phase > 0:
            parts = jnp.split(moe.astype(jnp.bfloat16), SIDE, axis=0)
    hidden = (resid.astype(jnp.float32) + moe).astype(jnp.bfloat16)
    attn_in = rms_scale(hidden, attn_gain).astype(jnp.bfloat16)
    kv_raw = jnp.dot(attn_in, w_kv, preferred_element_type=jnp.float32)
    latent = rms_scale(kv_raw[:, :KVL], kv_gain)
    rotated = rotate_half(kv_raw[:, KVL:], lengths)
    new_entry = jnp.concatenate([latent, rotated], axis=-1).astype(jnp.bfloat16)
    scores_old = (
        jnp.einsum("thc,tpc->thp", queries, cache, preferred_element_type=jnp.float32) * SCORE_SCALE
    )
    scores_new = (
        jnp.einsum("thc,tc->th", queries, new_entry, preferred_element_type=jnp.float32)
        * SCORE_SCALE
    )
    live_mask = jnp.arange(cache.shape[1], dtype=jnp.int32)[None, None, :] < lengths[:, None, None]
    scores_old = jnp.where(live_mask, scores_old, -jnp.inf)
    peak = jnp.maximum(jnp.max(scores_old, axis=2), scores_new)
    exp_old = jnp.exp(scores_old - peak[:, :, None])
    exp_new = jnp.exp(scores_new - peak)
    denom = jnp.sum(exp_old, axis=2) + exp_new
    probs_old = (exp_old / denom[:, :, None]).astype(jnp.bfloat16)
    probs_new = (exp_new / denom).astype(jnp.bfloat16)
    mixed = jnp.einsum(
        "thp,tpc->thc", probs_old, cache[:, :, :KVL], preferred_element_type=jnp.float32
    )
    mixed = mixed + probs_new.astype(jnp.float32)[:, :, None] * new_entry[:, None, :KVL].astype(
        jnp.float32
    )
    attn_out = mixed.astype(jnp.bfloat16)
    return (hidden, new_entry, attn_out)


def solution(mesh):
    placed = (
        P(("sec", "dev"), None),
        P(),
        P(("sec", "dev"), None),
        P(("sec", "dev"), None),
        P(None, ("sec", "dev")),
        P(None, ("sec", "dev")),
        P(("sec", "dev"), None),
        P(),
        P(),
        P(),
        P(("sec", "dev"), None, None),
        P(("sec", "dev")),
        P(("sec", "dev"), None, None),
    )
    return jax.shard_map(
        on_device,
        mesh=mesh,
        in_specs=placed,
        out_specs=(P(("sec", "dev"), None), P(("sec", "dev"), None), P(("sec", "dev"), None, None)),
        check_vma=False,
    )
```
